256 devices in a mesh: rows: 8 (over z), chan: 32 (over y, x, core).
Axes of the slice: x: 4, y: 4, z: 8, core: 2. Of those that a mesh axis runs over, the one named last changes fastest.
Arguments:
- features: float32 [256, 96, 256], P('chan', 'rows'), may hold values from -6 to 6
- weight_in: float32 [256, 3, 3, 256], P('chan'), may hold values from -0.125 to 0.125
- weight_out: float32 [256, 3, 3, 128], replicated, may hold values from -0.125 to 0.125
- cotangent: float32 [192, 512, 128], P('rows', 'chan'), may hold values from -6 to 6
Outputs:
- grad_features: float32 [256, 96, 256], P('chan', 'rows')
- grad_weight_in: float32 [256, 3, 3, 256], P('chan')
- grad_weight_out: float32 [256, 3, 3, 128], P('chan')
The draws below stay inside these ranges and needn't reach their ends.
All inputs are finite; a program needn't handle non-finite values.
Results may differ from the reference program's by a relative error of at most 0.00023.
Values sent between devices are 32-bit elements; how exact they have to be, the bound alone decides.
No kernel may reach another device: no remote copies, remote signals or barrier semaphores. Data moves between devices by JAX's collectives and lax.ppermute only.
A program may use at most 64 MiB of HBM per device.

```python
import jax
import jax.numpy as jnp
from jax import lax

C = 256
CO = 128
H = 96
WH = 256


def block_scale(rng, extent, shards, low, high):
    loudness, own = 1.0, jax.random.fold_in(rng, 6)
    for axis_at, parts in shards:
        draws = jnp.exp(jax.random.uniform(jax.random.fold_in(own, axis_at), (parts,), jnp.float32, low / len(shards), high / len(shards)))
        loudness = loudness * jnp.repeat(draws, extent[axis_at] // parts).reshape([-1 if axis == axis_at else 1 for axis in range(len(extent))])
    return loudness


def centred(own_key, shape, width, bound, split=(), held_as=jnp.bfloat16):
    result = width * jax.random.normal(own_key, shape, jnp.float32)
    if split:
        result = result * block_scale(own_key, shape, split, -0.22, 0.18)
    return jnp.clip(result, -bound, bound).astype(held_as)


def setup_inputs(seed: int = 0) -> dict:
    key_of = jax.random.split(jax.random.key(seed), 5)
    return {
        "features": centred(key_of[0], (C, H, WH), 1.0, 6.0, ((0, 32), (1, 8)), jnp.float32),
        "weight_in": centred(key_of[1], (C, 3, 3, C), (9 * C) ** -0.5, 0.125, ((0, 32),), jnp.float32),
        "weight_out": centred(key_of[2], (C, 3, 3, CO), (9 * C) ** -0.5, 0.125, (), jnp.float32),
        "cotangent": centred(key_of[3], (2 * H, 2 * WH, CO), 1.0, 6.0, ((0, 8), (1, 32)), jnp.float32),
    }


EXACT = lax.Precision.HIGHEST

def convolve(inputs, kernel):
    return lax.conv_general_dilated(inputs, kernel, (1, 1), ((1, 1), (1, 1)), dimension_numbers=('NCHW', 'OIHW', 'NCHW'), precision=EXACT)

def reference(features, weight_in, weight_out, cotangent):

    def forward(features, weight_in, weight_out):
        hidden = convolve(features[None], jnp.transpose(weight_in, (0, 3, 1, 2)))
        upper = jnp.repeat(jnp.repeat(hidden, 2, axis=2), 2, axis=3)
        active = upper * jax.nn.sigmoid(upper)
        output = convolve(active, jnp.transpose(weight_out, (3, 0, 1, 2)))
        return output[0]
    output, pullback = jax.vjp(forward, features, weight_in, weight_out)
    gradient = pullback(jnp.transpose(cotangent, (2, 0, 1)))
    grad_scale = (4.0 * H * WH) ** (-0.5)
    return (gradient[0], gradient[1] * grad_scale, gradient[2] * grad_scale)
```

```python
import jax
import jax.numpy as jnp
from jax import lax
from jax.experimental import pallas as pl
from jax.experimental.pallas import tpu as pltpu
from jax.sharding import PartitionSpec as P

BLOCK = 16
STEP = BLOCK + 2
ROWS = 24
FLAT = 512
PACK = 72
BACK = 88
F32, BF16 = jnp.float32, jnp.bfloat16
ANYWHERE = pltpu.CompilerParams(vmem_limit_bytes=40 * 1024 * 1024)
FULL = pl.BlockSpec(memory_space=pltpu.VMEM)
SCALAR = pl.BlockSpec(memory_space=pltpu.SMEM)


def halves(x):
    high = x.astype(BF16)
    return high, (x - high.astype(F32)).astype(BF16)


def product(a, b, dims):
    def one(x, y):
        return lax.dot_general(x, y, (dims, ((), ())), preferred_element_type=F32)

    return one(a[0], b[0]) + (one(a[0], b[1]) + one(a[1], b[0]))


NN, NT, TN = ((1,), (0,)), ((1,), (1,)), ((0,), (0,))


def pack_kernel(where, own, other, near, far, kernels, out, image, line):
    parity = where[0]
    image[...] = jnp.zeros_like(image)
    line[...] = jnp.zeros_like(line)
    inner = slice(128, 384)
    half = ROWS // 2
    for i in range(half):
        image[1 + half * parity + i, :, inner] = own[i]
        image[1 + half * (1 - parity) + i, :, inner] = other[i]
    image[(ROWS + 1) * parity, :, inner] = near[...]
    image[(ROWS + 1) * (1 - parity), :, inner] = far[...]
    for block in range(16):
        start = 127 + BLOCK * block
        for r in range(ROWS + 2):
            line[:, r * STEP : (r + 1) * STEP] = image[r, :, start : start + STEP]
        for q in range(4):
            tile = line[:, q * 128 : (q + 1) * 128]
            out[2 * block, q * 8 : q * 8 + 8, :] = tile
            out[2 * block + 1, q * 8 : q * 8 + 8, :] = tile
    for core in range(2):
        part = kernels[core]
        for block in range(16):
            out[2 * block + core, 32:PACK, :] = part


def window_kernel(where, own, other, near, far, weight, s_high, s_low, grad, image, sums):
    core = where[1]
    image[:, pl.ds(pl.multiple_of(8 + 16 * core, 8), 16), :] = own[...]
    image[:, pl.ds(pl.multiple_of(24 - 16 * core, 8), 16), :] = other[...]
    left = jnp.where(core == 0, near[...], far[...])
    right = jnp.where(core == 0, far[...], near[...])
    for r in range(2 * ROWS + 2):
        image[r, 7:8, :] = left[r : r + 1]
        image[r, 40:41, :] = right[r : r + 1]
    sums[...] = jnp.zeros_like(sums)

    def cells(r, start, count):
        return image[r, pl.ds(start, count, stride=2), :]

    def pairs(r, start, count):
        return cells(r, start, count) + cells(r, start + 1, count)

    even = [pairs(r, 7, 17) for r in range(2 * ROWS + 2)]
    odd = [pairs(r, 8, 16) for r in range(2 * ROWS + 2)]
    for r in range(ROWS + 1):
        at = r * STEP
        sums[at : at + 17, 0:128] = even[2 * r] + even[2 * r + 1]
        sums[at : at + 16, 128:256] = odd[2 * r] + odd[2 * r + 1]
        if r < ROWS:
            sums[at : at + 17, 256:384] = even[2 * r + 1] + even[2 * r + 2]
            sums[at : at + 16, 384:512] = odd[2 * r + 1] + odd[2 * r + 2]
    high, low = halves(sums[...])
    s_high[...] = high
    s_low[...] = low
    total = None
    for kind in range(4):
        lanes = slice(kind * 128, (kind + 1) * 128)
        taps = [t for t in range(9) if kind_of(t) == kind]
        left_side = jnp.concatenate([weight[t * 64 : (t + 1) * 64, :] for t in taps], axis=0)
        each = product(halves(left_side), (high[:, lanes], low[:, lanes]), NT)
        for i, t in enumerate(taps):
            term = each[i * 64 : (i + 1) * 64]
            if shift_of(t):
                term = pltpu.roll(term, FLAT - shift_of(t), 1)
            total = term if total is None else total + term
    grad[...] = total


def kind_of(t):
    return 2 * (t // 3 == 1) + (t % 3 == 1)


def shift_of(t):
    return STEP * (t // 3 == 0) + (t % 3 == 0)


def main_kernel(recv, s_high, s_low, grad, keep, out, x_high, x_low, w_high, w_low, g_high, g_low):
    for pair in range(16):
        for q in range(4):
            tile = jnp.concatenate(
                [recv[pl.ds((2 * pair + i) * PACK + q * 8, 8), :] for i in range(2)], axis=0
            )
            high, low = halves(tile)
            x_high[pair * 16 : pair * 16 + 16, q * 128 : q * 128 + 128] = high
            x_low[pair * 16 : pair * 16 + 16, q * 128 : q * 128 + 128] = low
    for t in range(9):
        for h in range(2):
            tile = jnp.concatenate(
                [recv[pl.ds(32 + j * 18 + t * 2 + h, 32, stride=PACK), :] for j in range(2)], axis=0
            )
            high, low = halves(tile)
            w_high[t * 64 : t * 64 + 64, h * 128 : h * 128 + 128] = high
            w_low[t * 64 : t * 64 + 64, h * 128 : h * 128 + 128] = low
    weights = (w_high[...], w_low[...])
    image = (x_high[...], x_low[...])
    each = product(weights, image, NN)
    hidden = each[0:64]
    for t in range(1, 9):
        hidden = hidden + pltpu.roll(each[t * 64 : t * 64 + 64], FLAT - ((t // 3) * STEP + t % 3), 1)
    inside = keep[...] > 0.0
    sigma = 1.0 / (1.0 + jnp.exp(-hidden))
    active = jnp.where(inside, hidden * sigma, 0.0)
    slope = sigma * (1.0 + hidden * (1.0 - sigma))
    gradient = jnp.where(inside, grad[...] * slope, 0.0)
    for t in range(9):
        shift = (t // 3) * STEP + t % 3
        moved = pltpu.roll(gradient, shift, 1) if shift else gradient
        high, low = halves(moved)
        g_high[t * 64 : t * 64 + 64, :] = high
        g_low[t * 64 : t * 64 + 64, :] = low
    moved = (g_high[...], g_low[...])
    into = product(moved, image, NT)
    for t in range(9):
        for h in range(2):
            for j in range(2):
                out[pl.ds(32 + j * 18 + t * 2 + h, 32, stride=BACK), :] = into[
                    t * 64 + j * 32 : t * 64 + j * 32 + 32, h * 128 : h * 128 + 128
                ]
    shifts = [0, 1, STEP, STEP + 1]
    spread = jnp.concatenate([pltpu.roll(active, s, 1) if s else active for s in shifts], axis=0)
    onto = product(halves(spread), (s_high[...], s_low[...]), NN)
    for t in range(9):
        at, kind = shifts.index(shift_of(t)) * 64, kind_of(t)
        for j in range(2):
            out[pl.ds(68 + j * 9 + t, 32, stride=BACK), :] = onto[
                at + j * 32 : at + j * 32 + 32, kind * 128 : kind * 128 + 128
            ]
    back = product(weights, moved, TN)
    for d in range(32):
        for q in range(4):
            out[pl.ds(d * BACK + q * 8, 8), :] = back[d * 8 : d * 8 + 8, q * 128 : q * 128 + 128]
    blank = jnp.zeros((2, 128), F32)
    for d in range(32):
        out[pl.ds(d * BACK + 86, 2), :] = blank


def gather_kernel(scale, where, recv, weights, mine, theirs, image, line):
    parity = where[0]
    for core in range(2):
        total = recv[core, 32:BACK, :]
        for block in range(1, 16):
            total = total + recv[2 * block + core, 32:BACK, :]
        total = total * scale
        for z in range(8):
            weights[z, core * 56 : core * 56 + 56, :] = total
    image[...] = jnp.zeros_like(image)
    for block in range(16):
        start = 127 + BLOCK * block
        for q in range(4):
            at = slice(q * 8, q * 8 + 8)
            line[:, q * 128 : q * 128 + 128] = recv[2 * block, at, :] + recv[2 * block + 1, at, :]
        for r in range(ROWS + 2):
            image[r, :, start : start + STEP] += line[:, r * STEP : (r + 1) * STEP]
    half = ROWS // 2 + 1
    for i in range(half):
        mine[i] = image[half * parity + i, :, 128:384]
        theirs[i] = image[half * (1 - parity) + i, :, 128:384]


def shape(*dims, dtype=F32):
    return jax.ShapeDtypeStruct(dims, dtype)


def call(kernel, outs, scalars, args, scratch, flops, moved):
    return pl.pallas_call(
        kernel,
        out_shape=outs,
        in_specs=[SCALAR] * scalars + [FULL] * (args - scalars),
        out_specs=jax.tree.map(lambda _: FULL, outs),
        scratch_shapes=scratch,
        compiler_params=ANYWHERE,
        cost_estimate=pl.CostEstimate(flops=flops, bytes_accessed=moved, transcendentals=0),
    )


def local(features, weight_in, weight_out, cotangent):
    z, d = lax.axis_index("rows"), lax.axis_index("chan")
    parity, core = z % 2, d % 2
    where = jnp.stack([parity, core]).astype(jnp.int32)
    scale = (4.0 * features.shape[1] * lax.axis_size("rows") * features.shape[2]) ** (-0.5)

    def partner(n):
        return [(i, i ^ 1) for i in range(n)]

    def beside(n):
        return [(i, i + 1) for i in range(1, n - 1, 2)] + [(i, i - 1) for i in range(2, n, 2)]

    def beyond(n):
        return [(i, i + 2) for i in range(1, n - 2, 2)] + [(i, i - 2) for i in range(2, n, 2)]

    lines = jnp.transpose(features, (1, 0, 2))
    edge_f = lax.dynamic_index_in_dim(lines, 11 * parity, 0, False)
    edge_c = lax.dynamic_index_in_dim(cotangent, 23 * parity, 0, False)
    edge = jnp.concatenate([edge_f[:, :128], edge_f[:, 128:], edge_c], axis=0)
    near = lax.ppermute(edge, "rows", beside(8))
    far = lax.ppermute(edge, "rows", beyond(8))
    other = lax.ppermute(lines, "rows", partner(8))
    near_f = jnp.concatenate([near[:8], near[8:16]], axis=1)
    far_f = jnp.concatenate([far[:8], far[8:16]], axis=1)
    mine = lax.dynamic_slice_in_dim(weight_in, 4 * parity, 4, 0).reshape(2, 36, 128)
    mine = jnp.pad(mine, ((0, 0), (0, PACK - 68), (0, 0)))
    packed = call(
        pack_kernel, shape(32, PACK, 128), 1, 6,
        [pltpu.VMEM((ROWS + 2, 8, 512), F32), pltpu.VMEM((8, FLAT), F32)], 10**6, 10**6,
    )(where, lines, other, near_f, far_f, mine)
    recv = lax.all_to_all(packed, "chan", 0, 0, tiled=True)

    other_c = lax.ppermute(cotangent, "rows", partner(8))
    flip = parity == 1
    tall = jnp.concatenate(
        [
            jnp.where(flip, far[16:], near[16:])[None],
            jnp.where(flip, other_c, cotangent),
            jnp.where(flip, cotangent, other_c),
            jnp.where(flip, near[16:], far[16:])[None],
        ],
        axis=0,
    )
    side = lax.ppermute(lax.dynamic_index_in_dim(tall, 15 * core, 1, False), "chan", beside(32))
    other_tall = lax.ppermute(tall, "chan", partner(32))
    other_side = lax.ppermute(side, "chan", partner(32))
    group = lax.dynamic_index_in_dim(weight_out.reshape(32, 4, 2, 9, 128), 2 * parity + core, 1, False)
    group = jnp.transpose(group, (2, 1, 0, 3)).reshape(576, 128)
    s_high, s_low, grad = call(
        window_kernel,
        (shape(FLAT, 512, dtype=BF16), shape(FLAT, 512, dtype=BF16), shape(64, FLAT)), 1, 6,
        [pltpu.VMEM((2 * ROWS + 2, 48, 128), F32), pltpu.VMEM((FLAT, 512), F32)],
        3 * 10**8, 3 * 10**6,
    )(where, tall, other_tall, side, other_side, group)

    at = lax.broadcasted_iota(jnp.int32, (64, FLAT), 1)
    keep = jnp.where((at % STEP < BLOCK) & (at < ROWS * STEP), 1.0, 0.0).astype(F32)
    sent = call(
        main_kernel, shape(32 * BACK, 128), 0, 5,
        [
            pltpu.VMEM((256, FLAT), BF16), pltpu.VMEM((256, FLAT), BF16),
            pltpu.VMEM((576, 256), BF16), pltpu.VMEM((576, 256), BF16),
            pltpu.VMEM((576, FLAT), BF16), pltpu.VMEM((576, FLAT), BF16),
        ],
        10**9, 5 * 10**6,
    )(recv.reshape(32 * PACK, 128), s_high, s_low, grad, keep)
    back = lax.all_to_all(sent.reshape(32, BACK, 128), "chan", 0, 0, tiled=True)

    sums, own, given = call(
        lambda *refs: gather_kernel(scale, *refs),
        (shape(8, 112, 128), shape(13, 8, 256), shape(13, 8, 256)), 1, 2,
        [pltpu.VMEM((ROWS + 2, 8, 512), F32), pltpu.VMEM((8, FLAT), F32)], 10**6, 2 * 10**6,
    )(where, back)
    own = own + lax.ppermute(given, "rows", partner(8))
    outer = lax.ppermute(
        lax.dynamic_index_in_dim(own, 12 * parity, 0, False), "rows", beside(8)
    )
    rows = lax.dynamic_slice_in_dim(own, 1 - parity, 12, 0)
    place = (jnp.arange(12) == 11 * parity)[:, None, None]
    rows = rows + jnp.where(place, outer[None], 0.0)
    grad_image = jnp.transpose(rows, (1, 0, 2))
    sums = lax.all_to_all(sums, "rows", 0, 0, tiled=True)
    sums = sums.reshape(4, 2, 2, 56, 128).sum(axis=0)
    grad_in = sums[:, :, :36].reshape(8, 3, 3, 256)
    grad_out = sums[:, :, 36:54].reshape(8, 3, 3, 128)
    return (grad_image, grad_in, grad_out)


def solution(mesh):
    return jax.shard_map(
        local,
        mesh=mesh,
        in_specs=(
            P("chan", "rows", None),
            P("chan", None, None, None),
            P(),
            P("rows", "chan", None),
        ),
        out_specs=(
            P("chan", "rows", None),
            P("chan", None, None, None),
            P("chan", None, None, None),
        ),
        check_vma=False,
    )
```

```python
import jax
import jax.numpy as jnp
from jax import lax
from jax.experimental import pallas as pl
from jax.experimental.pallas import tpu as pltpu
from jax.sharding import PartitionSpec as P

BLOCK = 16
STEP = BLOCK + 2
ROWS = 24
FLAT = 512
PACK = 40
BACK = 88
F32, BF16 = jnp.float32, jnp.bfloat16
GRANT = pltpu.CompilerParams(vmem_limit_bytes=20 * 1024 * 1024)
FULL = pl.BlockSpec(memory_space=pltpu.VMEM)


def halves(x):
    high = x.astype(BF16)
    return high, (x - high.astype(F32)).astype(BF16)


def product(a, b, dims):
    def one(x, y):
        return lax.dot_general(x, y, (dims, ((), ())), preferred_element_type=F32)

    return one(a[0], b[0]) + (one(a[0], b[1]) + one(a[1], b[0]))


NN, NT, TN = ((1,), (0,)), ((1,), (1,)), ((0,), (0,))


def prepare_kernel(features, cotangent, weight, edge, packed, part):
    parity = lax.axis_index("rows") % 2
    row = features[(ROWS // 2 - 1) * parity]
    edge[0:8, :] = row[:, :128]
    edge[8:16, :] = row[:, 128:]
    edge[16:32, :] = cotangent[(ROWS - 1) * parity]
    part[...] = jnp.zeros_like(part)
    for t in range(9):
        rows = jnp.where(parity == 0, weight[t, 0:4, :], weight[t, 4:8, :])
        for core in range(2):
            for h in range(2):
                at = (t * 2 + h) * 2
                part[core, at : at + 2, :] = rows[
                    2 * core : 2 * core + 2, h * 128 : h * 128 + 128
                ]
    for core in range(2):
        tile = part[core]
        for block in range(16):
            packed[2 * block + core] = tile


def pack_kernel(own, other, near, far, out, image, line):
    parity = lax.axis_index("rows") % 2
    image[...] = jnp.zeros_like(image)
    line[...] = jnp.zeros_like(line)
    inner = slice(128, 384)
    half = ROWS // 2
    for i in range(half):
        image[1 + half * parity + i, :, inner] = own[i]
        image[1 + half * (1 - parity) + i, :, inner] = other[i]
    for edge, at in ((near, parity), (far, 1 - parity)):
        image[(ROWS + 1) * at, :, 128:256] = edge[0:8]
        image[(ROWS + 1) * at, :, 256:384] = edge[8:16]
    for block in range(16):
        start = 127 + BLOCK * block
        for r in range(ROWS + 2):
            line[:, r * STEP : (r + 1) * STEP] = image[r, :, start : start + STEP]
        for q in range(4):
            tile = line[:, q * 128 : (q + 1) * 128]
            out[2 * block, q * 8 : q * 8 + 8, :] = tile
            out[2 * block + 1, q * 8 : q * 8 + 8, :] = tile


def column_kernel(own, other, near, far, tall, side):
    parity = lax.axis_index("rows") % 2
    core = lax.axis_index("chan") % 2
    tall[pl.ds(1 + ROWS * parity, ROWS)] = own[...]
    tall[pl.ds(1 + ROWS * (1 - parity), ROWS)] = other[...]
    tall[(2 * ROWS + 1) * parity] = near[16:32]
    tall[(2 * ROWS + 1) * (1 - parity)] = far[16:32]
    for r in range(2 * ROWS + 2):
        line = tall[r]
        side[r : r + 1, :] = jnp.where(core == 0, line[0:1], line[15:16])


def window_kernel(own, other, near, far, weight, s_high, s_low, grad, image, sums):
    core = lax.axis_index("chan") % 2
    group = 2 * (lax.axis_index("rows") % 2) + core
    image[:, pl.ds(pl.multiple_of(8 + 16 * core, 8), 16), :] = own[...]
    image[:, pl.ds(pl.multiple_of(24 - 16 * core, 8), 16), :] = other[...]
    left = jnp.where(core == 0, near[...], far[...])
    right = jnp.where(core == 0, far[...], near[...])
    for r in range(2 * ROWS + 2):
        image[r, 7:8, :] = left[r : r + 1]
        image[r, 40:41, :] = right[r : r + 1]
    sums[...] = jnp.zeros_like(sums)

    def cells(r, start, count):
        return image[r, pl.ds(start, count, stride=2), :]

    def pairs(r, start, count):
        return cells(r, start, count) + cells(r, start + 1, count)

    even = [pairs(r, 7, 17) for r in range(2 * ROWS + 2)]
    odd = [pairs(r, 8, 16) for r in range(2 * ROWS + 2)]
    for r in range(ROWS + 1):
        at = r * STEP
        sums[at : at + 17, 0:128] = even[2 * r] + even[2 * r + 1]
        sums[at : at + 16, 128:256] = odd[2 * r] + odd[2 * r + 1]
        if r < ROWS:
            sums[at : at + 17, 256:384] = even[2 * r + 1] + even[2 * r + 2]
            sums[at : at + 16, 384:512] = odd[2 * r + 1] + odd[2 * r + 2]
    high, low = halves(sums[...])
    s_high[...] = high
    s_low[...] = low
    total = None
    for kind in range(4):
        lanes = slice(kind * 128, (kind + 1) * 128)
        taps = [t for t in range(9) if kind_of(t) == kind]
        left_side = jnp.concatenate(
            [
                weight[pl.ds(t * 256 + 2 * group + j, 32, stride=8), :]
                for t in taps
                for j in range(2)
            ],
            axis=0,
        )
        each = product(halves(left_side), (high[:, lanes], low[:, lanes]), NT)
        for i, t in enumerate(taps):
            term = each[i * 64 : (i + 1) * 64]
            if shift_of(t):
                term = pltpu.roll(term, FLAT - shift_of(t), 1)
            total = term if total is None else total + term
    grad[...] = total


def kind_of(t):
    return 2 * (t // 3 == 1) + (t % 3 == 1)


def shift_of(t):
    return STEP * (t // 3 == 0) + (t % 3 == 0)


def main_kernel(recv, kernels, s_high, s_low, grad, out, x_high, x_low, w_high, w_low, g_high, g_low):
    for pair in range(16):
        for q in range(4):
            tile = jnp.concatenate(
                [recv[pl.ds((2 * pair + i) * 32 + q * 8, 8), :] for i in range(2)], axis=0
            )
            high, low = halves(tile)
            x_high[pair * 16 : pair * 16 + 16, q * 128 : q * 128 + 128] = high
            x_low[pair * 16 : pair * 16 + 16, q * 128 : q * 128 + 128] = low
    for t in range(9):
        for h in range(2):
            tile = jnp.concatenate(
                [kernels[pl.ds((t * 2 + h) * 2 + j, 32, stride=PACK), :] for j in range(2)], axis=0
            )
            high, low = halves(tile)
            w_high[t * 64 : t * 64 + 64, h * 128 : h * 128 + 128] = high
            w_low[t * 64 : t * 64 + 64, h * 128 : h * 128 + 128] = low
    weights = (w_high[...], w_low[...])
    image = (x_high[...], x_low[...])
    each = product(weights, image, NN)
    hidden = each[0:64]
    for t in range(1, 9):
        hidden = hidden + pltpu.roll(each[t * 64 : t * 64 + 64], FLAT - ((t // 3) * STEP + t % 3), 1)
    at = lax.broadcasted_iota(jnp.int32, (64, FLAT), 1)
    inside = (at % STEP < BLOCK) & (at < ROWS * STEP)
    sigma = 1.0 / (1.0 + jnp.exp(-hidden))
    active = jnp.where(inside, hidden * sigma, 0.0)
    slope = sigma * (1.0 + hidden * (1.0 - sigma))
    gradient = jnp.where(inside, grad[...] * slope, 0.0)
    for t in range(9):
        shift = (t // 3) * STEP + t % 3
        moved = pltpu.roll(gradient, shift, 1) if shift else gradient
        high, low = halves(moved)
        g_high[t * 64 : t * 64 + 64, :] = high
        g_low[t * 64 : t * 64 + 64, :] = low
    moved = (g_high[...], g_low[...])
    into = product(moved, image, NT)
    for t in range(9):
        for h in range(2):
            for j in range(2):
                out[pl.ds(32 + (t * 2 + h) * 2 + j, 32, stride=BACK), :] = into[
                    t * 64 + j * 32 : t * 64 + j * 32 + 32, h * 128 : h * 128 + 128
                ]
    shifts = [0, 1, STEP, STEP + 1]
    spread = jnp.concatenate([pltpu.roll(active, s, 1) if s else active for s in shifts], axis=0)
    onto = product(halves(spread), (s_high[...], s_low[...]), NN)
    for t in range(9):
        at, kind = shifts.index(shift_of(t)) * 64, kind_of(t)
        for j in range(2):
            out[pl.ds(68 + t * 2 + j, 32, stride=BACK), :] = onto[
                at + j * 32 : at + j * 32 + 32, kind * 128 : kind * 128 + 128
            ]
    back = product(weights, moved, TN)
    for d in range(32):
        for q in range(4):
            out[pl.ds(d * BACK + q * 8, 8), :] = back[d * 8 : d * 8 + 8, q * 128 : q * 128 + 128]
    blank = jnp.zeros((2, 128), F32)
    for d in range(32):
        out[pl.ds(d * BACK + 86, 2), :] = blank


def gather_kernel(scale, recv, weights, mine, theirs, beside, beyond, image, line, total, mixed):
    parity = lax.axis_index("rows") % 2
    mixed[...] = jnp.zeros_like(mixed)
    for core in range(2):
        each = recv[core, 32:BACK, :]
        for block in range(1, 16):
            each = each + recv[2 * block + core, 32:BACK, :]
        total[...] = each * scale
        for j in range(2):
            mixed[pl.ds(2 * core + j, 27, stride=4), :] = total[pl.ds(j, 27, stride=2), :]
    tile = mixed[...]
    for z in range(8):
        weights[z] = tile
    image[...] = jnp.zeros_like(image)
    for block in range(16):
        start = 127 + BLOCK * block
        for q in range(4):
            at = slice(q * 8, q * 8 + 8)
            line[:, q * 128 : q * 128 + 128] = recv[2 * block, at, :] + recv[2 * block + 1, at, :]
        for r in range(ROWS + 2):
            image[r, :, start : start + STEP] += line[:, r * STEP : (r + 1) * STEP]
    half = ROWS // 2
    for i in range(half):
        mine[i] = image[1 + half * parity + i, :, 128:384]
        theirs[i] = image[1 + half * (1 - parity) + i, :, 128:384]
    beside[...] = image[(ROWS + 1) * parity, :, 128:384]
    beyond[...] = image[(ROWS + 1) * (1 - parity), :, 128:384]


def final_kernel(recv, into, onto):
    sums = []
    for parity in range(2):
        sums.append((recv[parity] + recv[2 + parity]) + (recv[4 + parity] + recv[6 + parity]))
    for k in range(27):
        tile = jnp.concatenate([x[4 * k : 4 * k + 4] for x in sums], axis=0)
        if k < 18:
            into[k // 2, :, (k % 2) * 128 : (k % 2) * 128 + 128] = tile
        else:
            onto[k - 18] = tile


def shape(*dims, dtype=F32):
    return jax.ShapeDtypeStruct(dims, dtype)


def call(kernel, outs, args, scratch=(), flops=10**6, moved=10**6):
    return pl.pallas_call(
        kernel,
        out_shape=outs,
        in_specs=[FULL] * args,
        out_specs=jax.tree.map(lambda _: FULL, outs),
        scratch_shapes=list(scratch),
        compiler_params=GRANT,
        cost_estimate=pl.CostEstimate(flops=flops, bytes_accessed=moved, transcendentals=0),
    )


def partner(n):
    return [(i, i ^ 1) for i in range(n)]


def beside(n):
    return [(i, i + 1) for i in range(1, n - 1, 2)] + [(i, i - 1) for i in range(2, n, 2)]


def inward(n):
    return [(i, i + 2) for i in range(1, n - 2, 2)] + [(i, i - 2) for i in range(2, n, 2)]


def outward(n):
    return [(i, i + 2) for i in range(0, n - 2, 2)] + [(i, i - 2) for i in range(3, n, 2)]


def local(features, weight_in, weight_out, cotangent):
    parity = lax.axis_index("rows") % 2
    scale = (4.0 * features.shape[1] * lax.axis_size("rows") * features.shape[2]) ** (-0.5)
    wide = pltpu.VMEM((ROWS + 2, 8, 512), F32)
    flat = pltpu.VMEM((8, FLAT), F32)

    lines = jnp.transpose(features, (1, 0, 2))
    taps = jnp.transpose(weight_in, (1, 2, 0, 3)).reshape(9, 8, 256)
    edge, packed = call(
        prepare_kernel, (shape(32, 128), shape(32, PACK, 128)), 3, [pltpu.VMEM((2, PACK, 128), F32)]
    )(lines, cotangent, taps)
    kernels = lax.all_to_all(packed, "chan", 0, 0, tiled=True)
    near = lax.ppermute(edge, "rows", beside(8))
    far = lax.ppermute(edge, "rows", inward(8))
    other = lax.ppermute(lines, "rows", partner(8))
    other_c = lax.ppermute(cotangent, "rows", partner(8))
    packed = call(pack_kernel, shape(32, 32, 128), 4, [wide, flat])(lines, other, near, far)
    recv = lax.all_to_all(packed, "chan", 0, 0, tiled=True)

    tall, side = call(column_kernel, (shape(50, 16, 128), shape(50, 128)), 4)(
        cotangent, other_c, near, far
    )
    side = lax.ppermute(side, "chan", beside(32))
    other_tall = lax.ppermute(tall, "chan", partner(32))
    other_side = lax.ppermute(side, "chan", partner(32))
    s_high, s_low, grad = call(
        window_kernel,
        (shape(FLAT, 512, dtype=BF16), shape(FLAT, 512, dtype=BF16), shape(64, FLAT)), 5,
        [pltpu.VMEM((2 * ROWS + 2, 48, 128), F32), pltpu.VMEM((FLAT, 512), F32)],
        3 * 10**8, 3 * 10**6,
    )(tall, other_tall, side, other_side, jnp.transpose(weight_out, (1, 2, 0, 3)).reshape(2304, 128))

    sent = call(
        main_kernel, shape(32 * BACK, 128), 5,
        [
            pltpu.VMEM((256, FLAT), BF16), pltpu.VMEM((256, FLAT), BF16),
            pltpu.VMEM((576, 256), BF16), pltpu.VMEM((576, 256), BF16),
            pltpu.VMEM((576, FLAT), BF16), pltpu.VMEM((576, FLAT), BF16),
        ],
        10**9, 5 * 10**6,
    )(recv.reshape(1024, 128), kernels.reshape(32 * PACK, 128), s_high, s_low, grad)
    back = lax.all_to_all(sent.reshape(32, BACK, 128), "chan", 0, 0, tiled=True)

    sums, own, given, close, away = call(
        lambda *refs: gather_kernel(scale, *refs),
        (shape(8, 112, 128), shape(12, 8, 256), shape(12, 8, 256), shape(8, 256), shape(8, 256)), 1,
        [wide, flat, pltpu.VMEM((56, 128), F32), pltpu.VMEM((112, 128), F32)],
    )(back)
    given = lax.ppermute(given, "rows", partner(8))
    close = lax.ppermute(close, "rows", beside(8))
    away = lax.ppermute(away, "rows", outward(8))
    sums = lax.all_to_all(sums, "rows", 0, 0, tiled=True)
    place = (jnp.arange(12) == 11 * parity)[:, None, None]
    grad_image = jnp.transpose((own + given) + jnp.where(place, (close + away)[None], 0.0), (1, 0, 2))
    into, onto = call(final_kernel, (shape(9, 8, 256), shape(9, 8, 128)), 1)(sums)
    grad_in = jnp.transpose(into.reshape(3, 3, 8, 256), (2, 0, 1, 3))
    grad_out = jnp.transpose(onto.reshape(3, 3, 8, 128), (2, 0, 1, 3))
    return (grad_image, grad_in, grad_out)


def solution(mesh):
    return jax.shard_map(
        local,
        mesh=mesh,
        in_specs=(
            P("chan", "rows", None),
            P("chan", None, None, None),
            P(),
            P("rows", "chan", None),
        ),
        out_specs=(
            P("chan", "rows", None),
            P("chan", None, None, None),
            P("chan", None, None, None),
        ),
        check_vma=False,
    )
```

```python
import jax
import jax.numpy as jnp
from jax import lax
from jax.experimental import pallas as pl
from jax.experimental.pallas import tpu as pltpu
from jax.sharding import PartitionSpec as P

BLOCK = 16
STEP = BLOCK + 2
ROWS = 24
FINE = 2 * ROWS + 6
FLAT = 512
PACK = 40
BACK = 88
F32, BF16 = jnp.float32, jnp.bfloat16
GRANT, MOST = 20 * 1024 * 1024, 60 * 1024 * 1024
FULL = pl.BlockSpec(memory_space=pltpu.VMEM)


def halves(x):
    high = x.astype(BF16)
    return high, (x - high.astype(F32)).astype(BF16)


def product(a, b, dims):
    def one(x, y):
        return lax.dot_general(x, y, (dims, ((), ())), preferred_element_type=F32)

    return one(a[0], b[0]) + (one(a[0], b[1]) + one(a[1], b[0]))


NN, NT, TN = ((1,), (0,)), ((1,), (1,)), ((0,), (0,))


def prepare_kernel(features, cotangent, weight, edge, packed, lines, cells, taps, part, sems):
    parity = lax.axis_index("rows") % 2
    half = ROWS // 2
    copies = [
        pltpu.make_async_copy(weight, taps, sems.at[0]),
        pltpu.make_async_copy(features.at[pl.ds((half - 2) * parity, 2)], lines, sems.at[1]),
        pltpu.make_async_copy(cotangent.at[pl.ds((ROWS - 3) * parity, 3)], cells, sems.at[2]),
    ]
    for copy in copies:
        copy.start()
    part[...] = jnp.zeros_like(part)
    for copy in copies:
        copy.wait()
    for k in range(2):
        for h in range(2):
            at = (2 * k + h) * 8
            edge[at : at + 8, :] = lines[k, :, h * 128 : h * 128 + 128]
    for k in range(3):
        edge[32 + k * 16 : 48 + k * 16, :] = cells[k]
    for t in range(9):
        rows = jnp.where(parity == 0, taps[t, 0:4, :], taps[t, 4:8, :])
        for core in range(2):
            for h in range(2):
                at = (t * 2 + h) * 2
                part[core, at : at + 2, :] = rows[
                    2 * core : 2 * core + 2, h * 128 : h * 128 + 128
                ]
    for core in range(2):
        tile = part[core]
        for block in range(16):
            packed[2 * block + core] = tile


def pack_kernel(own, other, near, far, out, image, line):
    parity = lax.axis_index("rows") % 2
    image[...] = jnp.zeros_like(image)
    line[...] = jnp.zeros_like(line)
    inner = slice(128, 384)
    half = ROWS // 2
    for i in range(half):
        image[2 + half * parity + i, :, inner] = own[i]
        image[2 + half * (1 - parity) + i, :, inner] = other[i]
    for edge, at in ((near, parity), (far, 1 - parity)):
        for k in range(2):
            for h in range(2):
                rows = (2 * k + h) * 8
                image[(ROWS + 2) * at + k, :, 128 + h * 128 : 256 + h * 128] = edge[rows : rows + 8]
    for block in range(16):
        start = 127 + BLOCK * block
        for r in range(ROWS + 4):
            line[:, r * STEP : (r + 1) * STEP] = image[r, :, start : start + STEP]
        for q in range(4):
            tile = line[:, q * 128 : (q + 1) * 128]
            out[2 * block, q * 8 : q * 8 + 8, :] = tile
            out[2 * block + 1, q * 8 : q * 8 + 8, :] = tile


def column_kernel(own, other, near, far, tall, side):
    parity = lax.axis_index("rows") % 2
    core = lax.axis_index("chan") % 2
    tall[pl.ds(3 + ROWS * parity, ROWS)] = own[...]
    tall[pl.ds(3 + ROWS * (1 - parity), ROWS)] = other[...]
    for edge, at in ((near, parity), (far, 1 - parity)):
        for k in range(3):
            tall[(2 * ROWS + 3) * at + k] = edge[32 + 16 * k : 48 + 16 * k]
    for r in range(FINE):
        line = tall[r]
        side[r : r + 1, :] = jnp.where(core == 0, line[0:1], line[15:16])
    side[FINE : FINE + 2, :] = jnp.zeros((2, 128), F32)


def window_kernel(own, other, near, far, weight, s_high, s_low, grad, image, sums):
    core = lax.axis_index("chan") % 2
    group = 2 * (lax.axis_index("rows") % 2) + core
    image[:, pl.ds(pl.multiple_of(8 + 16 * core, 8), 16), :] = own[...]
    image[:, pl.ds(pl.multiple_of(24 - 16 * core, 8), 16), :] = other[...]
    left = jnp.where(core == 0, near[...], far[...])
    right = jnp.where(core == 0, far[...], near[...])
    for r in range(FINE):
        image[r, 7:8, :] = left[r : r + 1]
        image[r, 40:41, :] = right[r : r + 1]
    sums[...] = jnp.zeros_like(sums)

    def cells(r, start, count):
        return image[r, pl.ds(start, count, stride=2), :]

    def pairs(r, start, count):
        return cells(r, start, count) + cells(r, start + 1, count)

    even = [pairs(r, 7, 17) for r in range(FINE)]
    odd = [pairs(r, 8, 16) for r in range(FINE)]
    for r in range(ROWS + 3):
        at = r * STEP
        sums[at : at + 17, 0:128] = even[2 * r] + even[2 * r + 1]
        sums[at : at + 16, 128:256] = odd[2 * r] + odd[2 * r + 1]
        if r < ROWS + 2:
            sums[at : at + 17, 256:384] = even[2 * r + 1] + even[2 * r + 2]
            sums[at : at + 16, 384:512] = odd[2 * r + 1] + odd[2 * r + 2]
    high, low = halves(sums[...])
    s_high[...] = high
    s_low[...] = low
    total = None
    for kind in range(4):
        lanes = slice(kind * 128, (kind + 1) * 128)
        taps = [t for t in range(9) if kind_of(t) == kind]
        left_side = jnp.concatenate(
            [
                weight[pl.ds(t * 256 + 2 * group + j, 32, stride=8), :]
                for t in taps
                for j in range(2)
            ],
            axis=0,
        )
        each = product(halves(left_side), (high[:, lanes], low[:, lanes]), NT)
        for i, t in enumerate(taps):
            term = each[i * 64 : (i + 1) * 64]
            if shift_of(t):
                term = pltpu.roll(term, FLAT - shift_of(t), 1)
            total = term if total is None else total + term
    grad[...] = total


def kind_of(t):
    return 2 * (t // 3 == 1) + (t % 3 == 1)


def shift_of(t):
    return STEP * (t // 3 == 0) + (t % 3 == 0)


def main_kernel(recv, kernels, s_high, s_low, grad, out, x_high, x_low, w_high, w_low, g_high, g_low):
    for pair in range(16):
        for q in range(4):
            tile = jnp.concatenate(
                [recv[pl.ds((2 * pair + i) * 32 + q * 8, 8), :] for i in range(2)], axis=0
            )
            high, low = halves(tile)
            x_high[pair * 16 : pair * 16 + 16, q * 128 : q * 128 + 128] = high
            x_low[pair * 16 : pair * 16 + 16, q * 128 : q * 128 + 128] = low
    for t in range(9):
        for h in range(2):
            tile = jnp.concatenate(
                [kernels[pl.ds((t * 2 + h) * 2 + j, 32, stride=PACK), :] for j in range(2)], axis=0
            )
            high, low = halves(tile)
            w_high[t * 64 : t * 64 + 64, h * 128 : h * 128 + 128] = high
            w_low[t * 64 : t * 64 + 64, h * 128 : h * 128 + 128] = low
    weights = (w_high[...], w_low[...])
    image = (x_high[...], x_low[...])
    each = product(weights, image, NN)
    hidden = each[0:64]
    for t in range(1, 9):
        hidden = hidden + pltpu.roll(each[t * 64 : t * 64 + 64], FLAT - ((t // 3) * STEP + t % 3), 1)
    at = lax.broadcasted_iota(jnp.int32, (64, FLAT), 1)
    block = lax.axis_index("rows") // 2
    across = at % STEP < BLOCK
    inside = across & (at >= STEP) & (at < (ROWS + 1) * STEP)
    top = jnp.where(block == 0, STEP, 0)
    bottom = jnp.where(block == 3, (ROWS + 1) * STEP, (ROWS + 2) * STEP)
    around = across & (at >= top) & (at < bottom)
    sigma = 1.0 / (1.0 + jnp.exp(-hidden))
    active = jnp.where(inside, hidden * sigma, 0.0)
    slope = sigma * (1.0 + hidden * (1.0 - sigma))
    gradient = grad[...] * slope

    def stack(values, offset):
        for t in range(9):
            shift = ((t // 3) * STEP + t % 3 + offset) % FLAT
            high, low = halves(pltpu.roll(values, shift, 1) if shift else values)
            g_high[t * 64 : t * 64 + 64, :] = high
            g_low[t * 64 : t * 64 + 64, :] = low
        return g_high[...], g_low[...]

    moved = stack(jnp.where(inside, gradient, 0.0), 0)
    into = product(moved, image, NT)
    for t in range(9):
        for h in range(2):
            for j in range(2):
                out[pl.ds(32 + (t * 2 + h) * 2 + j, 32, stride=BACK), :] = into[
                    t * 64 + j * 32 : t * 64 + j * 32 + 32, h * 128 : h * 128 + 128
                ]
    shifts = [0, 1, STEP, STEP + 1]
    spread = jnp.concatenate([pltpu.roll(active, s, 1) if s else active for s in shifts], axis=0)
    onto = product(halves(spread), (s_high[...], s_low[...]), NN)
    for t in range(9):
        at, kind = shifts.index(shift_of(t)) * 64, kind_of(t)
        for j in range(2):
            out[pl.ds(68 + t * 2 + j, 32, stride=BACK), :] = onto[
                at + j * 32 : at + j * 32 + 32, kind * 128 : kind * 128 + 128
            ]
    back = product(weights, stack(jnp.where(around, gradient, 0.0), -2 * STEP), TN)
    for d in range(32):
        for q in range(4):
            out[pl.ds(d * BACK + q * 8, 8), :] = back[d * 8 : d * 8 + 8, q * 128 : q * 128 + 128]
    blank = jnp.zeros((2, 128), F32)
    for d in range(32):
        out[pl.ds(d * BACK + 86, 2), :] = blank


def gather_kernel(scale, recv, weights, mine, theirs, image, line, total, mixed):
    parity = lax.axis_index("rows") % 2
    mixed[...] = jnp.zeros_like(mixed)
    for core in range(2):
        each = recv[core, 32:BACK, :]
        for block in range(1, 16):
            each = each + recv[2 * block + core, 32:BACK, :]
        total[...] = each * scale
        for j in range(2):
            mixed[pl.ds(2 * core + j, 27, stride=4), :] = total[pl.ds(j, 27, stride=2), :]
    tile = mixed[...]
    for z in range(8):
        weights[z] = tile
    image[...] = jnp.zeros_like(image)
    for block in range(16):
        start = 127 + BLOCK * block
        for q in range(4):
            at = slice(q * 8, q * 8 + 8)
            line[:, q * 128 : q * 128 + 128] = recv[2 * block, at, :] + recv[2 * block + 1, at, :]
        for r in range(ROWS):
            image[r, :, start : start + STEP] += line[:, r * STEP : (r + 1) * STEP]
    half = ROWS // 2
    for i in range(half):
        mine[i] = image[half * parity + i, :, 128:384]
        theirs[i] = image[half * (1 - parity) + i, :, 128:384]


def final_kernel(recv, into, onto):
    sums = []
    for parity in range(2):
        sums.append((recv[parity] + recv[2 + parity]) + (recv[4 + parity] + recv[6 + parity]))
    for k in range(27):
        tile = jnp.concatenate([x[4 * k : 4 * k + 4] for x in sums], axis=0)
        if k < 18:
            into[k // 2, :, (k % 2) * 128 : (k % 2) * 128 + 128] = tile
        else:
            onto[k - 18] = tile


def shape(*dims, dtype=F32):
    return jax.ShapeDtypeStruct(dims, dtype)


def call(kernel, outs, args, scratch=(), flops=10**6, moved=10**6, specs=None, grant=GRANT):
    return pl.pallas_call(
        kernel,
        out_shape=outs,
        in_specs=specs or [FULL] * args,
        out_specs=jax.tree.map(lambda _: FULL, outs),
        scratch_shapes=list(scratch),
        compiler_params=pltpu.CompilerParams(vmem_limit_bytes=grant),
        cost_estimate=pl.CostEstimate(flops=flops, bytes_accessed=moved, transcendentals=0),
    )


def partner(n):
    return [(i, i ^ 1) for i in range(n)]


def beside(n):
    return [(i, i + 1) for i in range(1, n - 1, 2)] + [(i, i - 1) for i in range(2, n, 2)]


def inward(n):
    return [(i, i + 2) for i in range(1, n - 2, 2)] + [(i, i - 2) for i in range(2, n, 2)]


def local(features, weight_in, weight_out, cotangent):
    scale = (4.0 * features.shape[1] * lax.axis_size("rows") * features.shape[2]) ** (-0.5)
    flat = pltpu.VMEM((8, FLAT), F32)

    lines = jnp.transpose(features, (1, 0, 2))
    taps = jnp.transpose(weight_in, (1, 2, 0, 3)).reshape(9, 8, 256)
    edge, packed = call(
        prepare_kernel, (shape(80, 128), shape(32, PACK, 128)), 3,
        [
            pltpu.VMEM((2, 8, 256), F32), pltpu.VMEM((3, 16, 128), F32),
            pltpu.VMEM((9, 8, 256), F32), pltpu.VMEM((2, PACK, 128), F32),
            pltpu.SemaphoreType.DMA((3,)),
        ],
        specs=[pl.BlockSpec(memory_space=pltpu.HBM)] * 3, grant=MOST,
    )(lines, cotangent, taps)
    near = lax.ppermute(edge, "rows", beside(8))
    far = lax.ppermute(edge, "rows", inward(8))
    other = lax.ppermute(lines, "rows", partner(8))
    other_c = lax.ppermute(cotangent, "rows", partner(8))
    kernels = lax.all_to_all(packed, "chan", 0, 0, tiled=True)
    near, far, other, other_c, kernels = lax.optimization_barrier((near, far, other, other_c, kernels))
    packed = call(pack_kernel, shape(32, 32, 128), 4, [pltpu.VMEM((ROWS + 4, 8, 512), F32), flat])(
        lines, other, near, far
    )
    recv = lax.all_to_all(packed, "chan", 0, 0, tiled=True)

    tall, side = call(column_kernel, (shape(FINE, 16, 128), shape(FINE + 2, 128)), 4)(
        cotangent, other_c, near, far
    )
    near_side = lax.ppermute(side, "chan", beside(32))
    far_side = lax.ppermute(side, "chan", inward(32))
    other_tall = lax.ppermute(tall, "chan", partner(32))
    s_high, s_low, grad = call(
        window_kernel,
        (shape(FLAT, 512, dtype=BF16), shape(FLAT, 512, dtype=BF16), shape(64, FLAT)), 5,
        [pltpu.VMEM((FINE, 48, 128), F32), pltpu.VMEM((FLAT, 512), F32)],
        3 * 10**8, 3 * 10**6,
    )(tall, other_tall, near_side, far_side, jnp.transpose(weight_out, (1, 2, 0, 3)).reshape(2304, 128))

    sent = call(
        main_kernel, shape(32 * BACK, 128), 5,
        [
            pltpu.VMEM((256, FLAT), BF16), pltpu.VMEM((256, FLAT), BF16),
            pltpu.VMEM((576, 256), BF16), pltpu.VMEM((576, 256), BF16),
            pltpu.VMEM((576, FLAT), BF16), pltpu.VMEM((576, FLAT), BF16),
        ],
        10**9, 5 * 10**6,
    )(recv.reshape(1024, 128), kernels.reshape(32 * PACK, 128), s_high, s_low, grad)
    back = lax.all_to_all(sent.reshape(32, BACK, 128), "chan", 0, 0, tiled=True)

    sums, own, given = call(
        lambda *refs: gather_kernel(scale, *refs),
        (shape(8, 112, 128), shape(12, 8, 256), shape(12, 8, 256)), 1,
        [
            pltpu.VMEM((ROWS, 8, 512), F32), flat,
            pltpu.VMEM((56, 128), F32), pltpu.VMEM((112, 128), F32),
        ],
    )(back)
    given = lax.ppermute(given, "rows", partner(8))
    sums = lax.all_to_all(sums, "rows", 0, 0, tiled=True)
    grad_image = jnp.transpose(own + given, (1, 0, 2))
    into, onto = call(final_kernel, (shape(9, 8, 256), shape(9, 8, 128)), 1)(sums)
    grad_in = jnp.transpose(into.reshape(3, 3, 8, 256), (2, 0, 1, 3))
    grad_out = jnp.transpose(onto.reshape(3, 3, 8, 128), (2, 0, 1, 3))
    return (grad_image, grad_in, grad_out)


def solution(mesh):
    return jax.shard_map(
        local,
        mesh=mesh,
        in_specs=(
            P("chan", "rows", None),
            P("chan", None, None, None),
            P(),
            P("rows", "chan", None),
        ),
        out_specs=(
            P("chan", "rows", None),
            P("chan", None, None, None),
            P("chan", None, None, None),
        ),
        check_vma=False,
    )
```

```python
import jax
import jax.numpy as jnp
from jax import lax
from jax.experimental import pallas as pl
from jax.experimental.pallas import tpu as pltpu
from jax.sharding import PartitionSpec as P

BLOCK = 16
STEP = BLOCK + 2
ROWS = 24
FINE = 2 * ROWS + 6
FLAT = 512
PACK = 40
BACK = 56
F32, BF16 = jnp.float32, jnp.bfloat16
GRANT, MOST = 20 * 1024 * 1024, 60 * 1024 * 1024
FULL = pl.BlockSpec(memory_space=pltpu.VMEM)


def halves(x):
    high = x.astype(BF16)
    return high, (x - high.astype(F32)).astype(BF16)


def product(a, b, dims):
    def one(x, y):
        return lax.dot_general(x, y, (dims, ((), ())), preferred_element_type=F32)

    return one(a[0], b[0]) + (one(a[0], b[1]) + one(a[1], b[0]))


NN, NT, TN = ((1,), (0,)), ((1,), (1,)), ((0,), (0,))


def prepare_kernel(features, cotangent, weight, edge, packed, lines, cells, taps, part, sems):
    parity = lax.axis_index("rows") % 2
    half = ROWS // 2
    copies = [
        pltpu.make_async_copy(weight, taps, sems.at[0]),
        pltpu.make_async_copy(features.at[pl.ds((half - 2) * parity, 2)], lines, sems.at[1]),
        pltpu.make_async_copy(cotangent.at[pl.ds((ROWS - 3) * parity, 3)], cells, sems.at[2]),
    ]
    for copy in copies:
        copy.start()
    part[...] = jnp.zeros_like(part)
    for copy in copies:
        copy.wait()
    for k in range(2):
        for h in range(2):
            at = (2 * k + h) * 8
            edge[at : at + 8, :] = lines[k, :, h * 128 : h * 128 + 128]
    for k in range(3):
        edge[32 + k * 16 : 48 + k * 16, :] = cells[k]
    for t in range(9):
        rows = jnp.where(parity == 0, taps[t, 0:4, :], taps[t, 4:8, :])
        for core in range(2):
            for h in range(2):
                at = (t * 2 + h) * 2
                part[core, at : at + 2, :] = rows[
                    2 * core : 2 * core + 2, h * 128 : h * 128 + 128
                ]
    for core in range(2):
        tile = part[core]
        for block in range(16):
            packed[2 * block + core] = tile


def pack_kernel(own, other, near, far, out, image, line):
    parity = lax.axis_index("rows") % 2
    image[...] = jnp.zeros_like(image)
    line[...] = jnp.zeros_like(line)
    inner = slice(128, 384)
    half = ROWS // 2
    for i in range(half):
        image[2 + half * parity + i, :, inner] = own[i]
        image[2 + half * (1 - parity) + i, :, inner] = other[i]
    for edge, at in ((near, parity), (far, 1 - parity)):
        for k in range(2):
            for h in range(2):
                rows = (2 * k + h) * 8
                image[(ROWS + 2) * at + k, :, 128 + h * 128 : 256 + h * 128] = edge[rows : rows + 8]
    for block in range(16):
        start = 127 + BLOCK * block
        for r in range(ROWS + 4):
            line[:, r * STEP : (r + 1) * STEP] = image[r, :, start : start + STEP]
        for q in range(4):
            tile = line[:, q * 128 : (q + 1) * 128]
            out[2 * block, q * 8 : q * 8 + 8, :] = tile
            out[2 * block + 1, q * 8 : q * 8 + 8, :] = tile


def column_kernel(own, other, near, far, tall, side):
    parity = lax.axis_index("rows") % 2
    core = lax.axis_index("chan") % 2
    tall[pl.ds(3 + ROWS * parity, ROWS)] = own[...]
    tall[pl.ds(3 + ROWS * (1 - parity), ROWS)] = other[...]
    for edge, at in ((near, parity), (far, 1 - parity)):
        for k in range(3):
            tall[(2 * ROWS + 3) * at + k] = edge[32 + 16 * k : 48 + 16 * k]
    for r in range(FINE):
        line = tall[r]
        side[r : r + 1, :] = jnp.where(core == 0, line[0:1], line[15:16])
    side[FINE : FINE + 2, :] = jnp.zeros((2, 128), F32)


def window_kernel(own, other, near, far, weight, s_high, s_low, grad, image, sums):
    core = lax.axis_index("chan") % 2
    group = 2 * (lax.axis_index("rows") % 2) + core
    image[:, pl.ds(pl.multiple_of(8 + 16 * core, 8), 16), :] = own[...]
    image[:, pl.ds(pl.multiple_of(24 - 16 * core, 8), 16), :] = other[...]
    left = jnp.where(core == 0, near[...], far[...])
    right = jnp.where(core == 0, far[...], near[...])
    for r in range(FINE):
        image[r, 7:8, :] = left[r : r + 1]
        image[r, 40:41, :] = right[r : r + 1]
    sums[...] = jnp.zeros_like(sums)

    def cells(r, start, count):
        return image[r, pl.ds(start, count, stride=2), :]

    def pairs(r, start, count):
        return cells(r, start, count) + cells(r, start + 1, count)

    even = [pairs(r, 7, 17) for r in range(FINE)]
    odd = [pairs(r, 8, 16) for r in range(FINE)]
    for r in range(ROWS + 3):
        at = r * STEP
        sums[at : at + 17, 0:128] = even[2 * r] + even[2 * r + 1]
        sums[at : at + 16, 128:256] = odd[2 * r] + odd[2 * r + 1]
        if r < ROWS + 2:
            sums[at : at + 17, 256:384] = even[2 * r + 1] + even[2 * r + 2]
            sums[at : at + 16, 384:512] = odd[2 * r + 1] + odd[2 * r + 2]
    high, low = halves(sums[...])
    s_high[...] = high
    s_low[...] = low
    total = None
    for kind in range(4):
        lanes = slice(kind * 128, (kind + 1) * 128)
        taps = [t for t in range(9) if kind_of(t) == kind]
        left_side = jnp.concatenate(
            [
                weight[pl.ds(t * 256 + 2 * group + j, 32, stride=8), :]
                for t in taps
                for j in range(2)
            ],
            axis=0,
        )
        each = product(halves(left_side), (high[:, lanes], low[:, lanes]), NT)
        for i, t in enumerate(taps):
            term = each[i * 64 : (i + 1) * 64]
            if shift_of(t):
                term = pltpu.roll(term, FLAT - shift_of(t), 1)
            total = term if total is None else total + term
    grad[...] = total


def kind_of(t):
    return 2 * (t // 3 == 1) + (t % 3 == 1)


def shift_of(t):
    return STEP * (t // 3 == 0) + (t % 3 == 0)


def main_kernel(recv, kernels, s_high, s_low, grad, out, mine, theirs, x_high, x_low, w_high, w_low, g_high, g_low):
    for pair in range(16):
        for q in range(4):
            tile = jnp.concatenate(
                [recv[pl.ds((2 * pair + i) * 32 + q * 8, 8), :] for i in range(2)], axis=0
            )
            high, low = halves(tile)
            x_high[pair * 16 : pair * 16 + 16, q * 128 : q * 128 + 128] = high
            x_low[pair * 16 : pair * 16 + 16, q * 128 : q * 128 + 128] = low
    for t in range(9):
        for h in range(2):
            tile = jnp.concatenate(
                [kernels[pl.ds((t * 2 + h) * 2 + j, 32, stride=PACK), :] for j in range(2)], axis=0
            )
            high, low = halves(tile)
            w_high[t * 64 : t * 64 + 64, h * 128 : h * 128 + 128] = high
            w_low[t * 64 : t * 64 + 64, h * 128 : h * 128 + 128] = low
    weights = (w_high[...], w_low[...])
    image = (x_high[...], x_low[...])
    each = product(weights, image, NN)
    hidden = each[0:64]
    for t in range(1, 9):
        hidden = hidden + pltpu.roll(each[t * 64 : t * 64 + 64], FLAT - ((t // 3) * STEP + t % 3), 1)
    at = lax.broadcasted_iota(jnp.int32, (64, FLAT), 1)
    block = lax.axis_index("rows") // 2
    across = at % STEP < BLOCK
    inside = across & (at >= STEP) & (at < (ROWS + 1) * STEP)
    top = jnp.where(block == 0, STEP, 0)
    bottom = jnp.where(block == 3, (ROWS + 1) * STEP, (ROWS + 2) * STEP)
    around = across & (at >= top) & (at < bottom)
    sigma = 1.0 / (1.0 + jnp.exp(-hidden))
    active = jnp.where(inside, hidden * sigma, 0.0)
    slope = sigma * (1.0 + hidden * (1.0 - sigma))
    gradient = grad[...] * slope

    def stack(values, offset):
        for t in range(9):
            shift = ((t // 3) * STEP + t % 3 + offset) % FLAT
            high, low = halves(pltpu.roll(values, shift, 1) if shift else values)
            g_high[t * 64 : t * 64 + 64, :] = high
            g_low[t * 64 : t * 64 + 64, :] = low
        return g_high[...], g_low[...]

    moved = stack(jnp.where(inside, gradient, 0.0), 0)
    into = product(moved, image, NT)
    for t in range(9):
        for h in range(2):
            for j in range(2):
                out[pl.ds((t * 2 + h) * 2 + j, 32, stride=BACK), :] = into[
                    t * 64 + j * 32 : t * 64 + j * 32 + 32, h * 128 : h * 128 + 128
                ]
    shifts = [0, 1, STEP, STEP + 1]
    spread = jnp.concatenate([pltpu.roll(active, s, 1) if s else active for s in shifts], axis=0)
    onto = product(halves(spread), (s_high[...], s_low[...]), NN)
    for t in range(9):
        at, kind = shifts.index(shift_of(t)) * 64, kind_of(t)
        for j in range(2):
            out[pl.ds(36 + t * 2 + j, 32, stride=BACK), :] = onto[
                at + j * 32 : at + j * 32 + 32, kind * 128 : kind * 128 + 128
            ]
    back = product(weights, stack(jnp.where(around, gradient, 0.0), -2 * STEP), TN)
    half = ROWS // 2 * STEP
    first = lax.axis_index("rows") % 2 == 0
    upper, lower = back[:, 0:256], pltpu.roll(back, FLAT - half, 1)[:, 0:256]
    for dst, part in (
        (mine, jnp.where(first, upper, lower)),
        (theirs, jnp.where(first, lower, upper)),
    ):
        for d in range(32):
            for q in range(2):
                dst[pl.ds(d * 16 + q * 8, 8), :] = part[d * 8 : d * 8 + 8, q * 128 : q * 128 + 128]
    blank = jnp.zeros((2, 128), F32)
    for d in range(32):
        out[pl.ds(d * BACK + 54, 2), :] = blank


def weights_kernel(scale, recv, mixed, total):
    mixed[...] = jnp.zeros_like(mixed)
    for core in range(2):
        each = recv[core]
        for block in range(1, 16):
            each = each + recv[2 * block + core]
        total[...] = each * scale
        for j in range(2):
            mixed[pl.ds(2 * core + j, 27, stride=4), :] = total[pl.ds(j, 27, stride=2), :]


def final_kernel(own, other, into, onto):
    first = lax.axis_index("rows") % 2 == 0
    sums = (
        jnp.where(first, own[...], other[...]),
        jnp.where(first, other[...], own[...]),
    )
    for k in range(27):
        tile = jnp.concatenate([x[4 * k : 4 * k + 4] for x in sums], axis=0)
        if k < 18:
            into[k // 2, :, (k % 2) * 128 : (k % 2) * 128 + 128] = tile
        else:
            onto[k - 18] = tile


def image_kernel(recv, out, image, line):
    image[...] = jnp.zeros_like(image)
    for block in range(16):
        start = 127 + BLOCK * block
        for q in range(2):
            at = slice(q * 8, q * 8 + 8)
            line[:, q * 128 : q * 128 + 128] = recv[2 * block, at, :] + recv[2 * block + 1, at, :]
        for r in range(ROWS // 2):
            image[r, :, start : start + STEP] += line[:, r * STEP : (r + 1) * STEP]
    for r in range(ROWS // 2):
        out[r] = image[r, :, 128:384]


def shape(*dims, dtype=F32):
    return jax.ShapeDtypeStruct(dims, dtype)


def call(kernel, outs, args, scratch=(), flops=10**6, moved=10**6, specs=None, grant=GRANT):
    return pl.pallas_call(
        kernel,
        out_shape=outs,
        in_specs=specs or [FULL] * args,
        out_specs=jax.tree.map(lambda _: FULL, outs),
        scratch_shapes=list(scratch),
        compiler_params=pltpu.CompilerParams(vmem_limit_bytes=grant),
        cost_estimate=pl.CostEstimate(flops=flops, bytes_accessed=moved, transcendentals=0),
    )


def partner(n):
    return [(i, i ^ 1) for i in range(n)]


def beside(n):
    return [(i, i + 1) for i in range(1, n - 1, 2)] + [(i, i - 1) for i in range(2, n, 2)]


def inward(n):
    return [(i, i + 2) for i in range(1, n - 2, 2)] + [(i, i - 2) for i in range(2, n, 2)]


def shifted(n, by):
    return [(i, (i + by) % n) for i in range(n)]


def local(features, weight_in, weight_out, cotangent):
    scale = (4.0 * features.shape[1] * lax.axis_size("rows") * features.shape[2]) ** (-0.5)
    flat = pltpu.VMEM((8, FLAT), F32)

    lines = jnp.transpose(features, (1, 0, 2))
    taps = jnp.transpose(weight_in, (1, 2, 0, 3)).reshape(9, 8, 256)
    edge, packed = call(
        prepare_kernel, (shape(80, 128), shape(32, PACK, 128)), 3,
        [
            pltpu.VMEM((2, 8, 256), F32), pltpu.VMEM((3, 16, 128), F32),
            pltpu.VMEM((9, 8, 256), F32), pltpu.VMEM((2, PACK, 128), F32),
            pltpu.SemaphoreType.DMA((3,)),
        ],
        specs=[pl.BlockSpec(memory_space=pltpu.HBM)] * 3, grant=MOST,
    )(lines, cotangent, taps)
    near = lax.ppermute(edge, "rows", beside(8))
    far = lax.ppermute(edge, "rows", inward(8))
    other = lax.ppermute(lines, "rows", partner(8))
    other_c = lax.ppermute(cotangent, "rows", partner(8))
    kernels = lax.all_to_all(packed, "chan", 0, 0, tiled=True)
    near, far, other, other_c, kernels = lax.optimization_barrier((near, far, other, other_c, kernels))
    packed = call(pack_kernel, shape(32, 32, 128), 4, [pltpu.VMEM((ROWS + 4, 8, 512), F32), flat])(
        lines, other, near, far
    )
    recv = lax.all_to_all(packed, "chan", 0, 0, tiled=True)

    tall, side = call(column_kernel, (shape(FINE, 16, 128), shape(FINE + 2, 128)), 4)(
        cotangent, other_c, near, far
    )
    near_side = lax.ppermute(side, "chan", beside(32))
    far_side = lax.ppermute(side, "chan", inward(32))
    other_tall = lax.ppermute(tall, "chan", partner(32))
    s_high, s_low, grad = call(
        window_kernel,
        (shape(FLAT, 512, dtype=BF16), shape(FLAT, 512, dtype=BF16), shape(64, FLAT)), 5,
        [pltpu.VMEM((FINE, 48, 128), F32), pltpu.VMEM((FLAT, 512), F32)],
        3 * 10**8, 3 * 10**6,
    )(tall, other_tall, near_side, far_side, jnp.transpose(weight_out, (1, 2, 0, 3)).reshape(2304, 128))

    sent, own, given = call(
        main_kernel, (shape(32 * BACK, 128), shape(512, 128), shape(512, 128)), 5,
        [
            pltpu.VMEM((256, FLAT), BF16), pltpu.VMEM((256, FLAT), BF16),
            pltpu.VMEM((576, 256), BF16), pltpu.VMEM((576, 256), BF16),
            pltpu.VMEM((576, FLAT), BF16), pltpu.VMEM((576, FLAT), BF16),
        ],
        10**9, 5 * 10**6,
    )(recv.reshape(1024, 128), kernels.reshape(32 * PACK, 128), s_high, s_low, grad)
    given = lax.ppermute(given, "rows", partner(8))
    back = lax.all_to_all(sent.reshape(32, BACK, 128), "chan", 0, 0, tiled=True)
    given, back = lax.optimization_barrier((given, back))
    mixed = call(lambda *refs: weights_kernel(scale, *refs), shape(112, 128), 1, [pltpu.VMEM((56, 128), F32)])(
        back
    )
    left = lax.ppermute(mixed, "rows", shifted(8, 2))
    right = lax.ppermute(mixed, "rows", shifted(8, 6))
    opposite = lax.ppermute(mixed, "rows", shifted(8, 4))
    image = lax.all_to_all((own + given).reshape(32, 16, 128), "chan", 0, 0, tiled=True)
    mixed = (mixed + opposite) + (left + right)
    counter = lax.ppermute(mixed, "rows", partner(8))
    into, onto = call(final_kernel, (shape(9, 8, 256), shape(9, 8, 128)), 2)(mixed, counter)
    rows = call(
        image_kernel, shape(12, 8, 256), 1, [pltpu.VMEM((12, 8, 512), F32), pltpu.VMEM((8, 256), F32)]
    )(image)
    grad_image = jnp.transpose(rows, (1, 0, 2))
    grad_in = jnp.transpose(into.reshape(3, 3, 8, 256), (2, 0, 1, 3))
    grad_out = jnp.transpose(onto.reshape(3, 3, 8, 128), (2, 0, 1, 3))
    return (grad_image, grad_in, grad_out)


def solution(mesh):
    return jax.shard_map(
        local,
        mesh=mesh,
        in_specs=(
            P("chan", "rows", None),
            P("chan", None, None, None),
            P(),
            P("rows", "chan", None),
        ),
        out_specs=(
            P("chan", "rows", None),
            P("chan", None, None, None),
            P("chan", None, None, None),
        ),
        check_vma=False,
    )
```

```python
import jax
import jax.numpy as jnp
from jax import lax
from jax.experimental import pallas as pl
from jax.experimental.pallas import tpu as pltpu
from jax.sharding import PartitionSpec as P

BLOCK = 16
STEP = BLOCK + 2
ROWS = 24
FINE = 2 * ROWS + 6
FLAT = 512
PACK = 40
BACK = 56
F32, BF16 = jnp.float32, jnp.bfloat16
GRANT, MOST = 20 * 1024 * 1024, 60 * 1024 * 1024
FULL = pl.BlockSpec(memory_space=pltpu.VMEM)


def halves(x):
    high = x.astype(BF16)
    return high, (x - high.astype(F32)).astype(BF16)


def product(a, b, dims):
    def one(x, y):
        return lax.dot_general(x, y, (dims, ((), ())), preferred_element_type=F32)

    return one(a[0], b[0]) + (one(a[0], b[1]) + one(a[1], b[0]))


NN, NT, TN = ((1,), (0,)), ((1,), (1,)), ((0,), (0,))


def prepare_kernel(features, cotangent, weight, edge, packed, lines, cells, taps, part, sems):
    parity = lax.axis_index("rows") % 2
    half = ROWS // 2
    copies = [
        pltpu.make_async_copy(weight, taps, sems.at[0]),
        pltpu.make_async_copy(features.at[pl.ds((half - 2) * parity, 2)], lines, sems.at[1]),
        pltpu.make_async_copy(cotangent.at[pl.ds((ROWS - 3) * parity, 3)], cells, sems.at[2]),
    ]
    for copy in copies:
        copy.start()
    part[...] = jnp.zeros_like(part)
    for copy in copies:
        copy.wait()
    for k in range(2):
        for h in range(2):
            at = (2 * k + h) * 8
            edge[at : at + 8, :] = lines[k, :, h * 128 : h * 128 + 128]
    for k in range(3):
        edge[32 + k * 16 : 48 + k * 16, :] = cells[k]
    for t in range(9):
        rows = jnp.where(parity == 0, taps[t, 0:4, :], taps[t, 4:8, :])
        for core in range(2):
            for h in range(2):
                at = (t * 2 + h) * 2
                part[core, at : at + 2, :] = rows[
                    2 * core : 2 * core + 2, h * 128 : h * 128 + 128
                ]
    for core in range(2):
        tile = part[core]
        for block in range(16):
            packed[2 * block + core] = tile


def pack_kernel(own, other, near, far, out, image, line):
    parity = lax.axis_index("rows") % 2
    image[...] = jnp.zeros_like(image)
    line[...] = jnp.zeros_like(line)
    inner = slice(128, 384)
    half = ROWS // 2
    for i in range(half):
        image[2 + half * parity + i, :, inner] = own[i]
        image[2 + half * (1 - parity) + i, :, inner] = other[i]
    for edge, at in ((near, parity), (far, 1 - parity)):
        for k in range(2):
            for h in range(2):
                rows = (2 * k + h) * 8
                image[(ROWS + 2) * at + k, :, 128 + h * 128 : 256 + h * 128] = edge[rows : rows + 8]
    for block in range(16):
        start = 127 + BLOCK * block
        for r in range(ROWS + 4):
            line[:, r * STEP : (r + 1) * STEP] = image[r, :, start : start + STEP]
        for q in range(4):
            tile = line[:, q * 128 : (q + 1) * 128]
            out[2 * block, q * 8 : q * 8 + 8, :] = tile
            out[2 * block + 1, q * 8 : q * 8 + 8, :] = tile


def column_kernel(own, other, near, far, tall, side):
    parity = lax.axis_index("rows") % 2
    core = lax.axis_index("chan") % 2
    tall[pl.ds(3 + ROWS * parity, ROWS)] = own[...]
    tall[pl.ds(3 + ROWS * (1 - parity), ROWS)] = other[...]
    for edge, at in ((near, parity), (far, 1 - parity)):
        for k in range(3):
            tall[(2 * ROWS + 3) * at + k] = edge[32 + 16 * k : 48 + 16 * k]
    for r in range(FINE):
        line = tall[r]
        side[r : r + 1, :] = jnp.where(core == 0, line[0:1], line[15:16])
    side[FINE : FINE + 2, :] = jnp.zeros((2, 128), F32)


def windows(own, other, near, far, weight, sums, image):
    core = lax.axis_index("chan") % 2
    group = 2 * (lax.axis_index("rows") % 2) + core
    image[:, pl.ds(pl.multiple_of(8 + 16 * core, 8), 16), :] = own[...]
    image[:, pl.ds(pl.multiple_of(24 - 16 * core, 8), 16), :] = other[...]
    left = jnp.where(core == 0, near[...], far[...])
    right = jnp.where(core == 0, far[...], near[...])
    for r in range(FINE):
        image[r, 7:8, :] = left[r : r + 1]
        image[r, 40:41, :] = right[r : r + 1]
    sums[...] = jnp.zeros_like(sums)

    def cells(r, start, count):
        return image[r, pl.ds(start, count, stride=2), :]

    def pairs(r, start, count):
        return cells(r, start, count) + cells(r, start + 1, count)

    even = [pairs(r, 7, 17) for r in range(FINE)]
    odd = [pairs(r, 8, 16) for r in range(FINE)]
    for r in range(ROWS + 3):
        at = r * STEP
        sums[at : at + 17, 0:128] = even[2 * r] + even[2 * r + 1]
        sums[at : at + 16, 128:256] = odd[2 * r] + odd[2 * r + 1]
        if r < ROWS + 2:
            sums[at : at + 17, 256:384] = even[2 * r + 1] + even[2 * r + 2]
            sums[at : at + 16, 384:512] = odd[2 * r + 1] + odd[2 * r + 2]
    high, low = halves(sums[...])
    total = None
    for kind in range(4):
        lanes = slice(kind * 128, (kind + 1) * 128)
        taps = [t for t in range(9) if kind_of(t) == kind]
        left_side = jnp.concatenate(
            [
                weight[pl.ds(t * 256 + 2 * group + j, 32, stride=8), :]
                for t in taps
                for j in range(2)
            ],
            axis=0,
        )
        each = product(halves(left_side), (high[:, lanes], low[:, lanes]), NT)
        for i, t in enumerate(taps):
            term = each[i * 64 : (i + 1) * 64]
            if shift_of(t):
                term = pltpu.roll(term, FLAT - shift_of(t), 1)
            total = term if total is None else total + term
    return (high, low), total


def kind_of(t):
    return 2 * (t // 3 == 1) + (t % 3 == 1)


def shift_of(t):
    return STEP * (t // 3 == 0) + (t % 3 == 0)


def main_kernel(
    recv, kernels, own, other, near, far, weight, out, mine, theirs,
    cells, sums, x_high, x_low, w_high, w_low, g_high, g_low,
):
    parts, grad = windows(own, other, near, far, weight, sums, cells)
    for pair in range(16):
        for q in range(4):
            tile = jnp.concatenate(
                [recv[pl.ds((2 * pair + i) * 32 + q * 8, 8), :] for i in range(2)], axis=0
            )
            high, low = halves(tile)
            x_high[pair * 16 : pair * 16 + 16, q * 128 : q * 128 + 128] = high
            x_low[pair * 16 : pair * 16 + 16, q * 128 : q * 128 + 128] = low
    for t in range(9):
        for h in range(2):
            tile = jnp.concatenate(
                [kernels[pl.ds((t * 2 + h) * 2 + j, 32, stride=PACK), :] for j in range(2)], axis=0
            )
            high, low = halves(tile)
            w_high[t * 64 : t * 64 + 64, h * 128 : h * 128 + 128] = high
            w_low[t * 64 : t * 64 + 64, h * 128 : h * 128 + 128] = low
    weights = (w_high[...], w_low[...])
    image = (x_high[...], x_low[...])
    each = product(weights, image, NN)
    hidden = each[0:64]
    for t in range(1, 9):
        hidden = hidden + pltpu.roll(each[t * 64 : t * 64 + 64], FLAT - ((t // 3) * STEP + t % 3), 1)
    at = lax.broadcasted_iota(jnp.int32, (64, FLAT), 1)
    block = lax.axis_index("rows") // 2
    across = at % STEP < BLOCK
    inside = across & (at >= STEP) & (at < (ROWS + 1) * STEP)
    top = jnp.where(block == 0, STEP, 0)
    bottom = jnp.where(block == 3, (ROWS + 1) * STEP, (ROWS + 2) * STEP)
    around = across & (at >= top) & (at < bottom)
    sigma = 1.0 / (1.0 + jnp.exp(-hidden))
    active = jnp.where(inside, hidden * sigma, 0.0)
    slope = sigma * (1.0 + hidden * (1.0 - sigma))
    gradient = grad * slope

    def stack(values, offset):
        for t in range(9):
            shift = ((t // 3) * STEP + t % 3 + offset) % FLAT
            high, low = halves(pltpu.roll(values, shift, 1) if shift else values)
            g_high[t * 64 : t * 64 + 64, :] = high
            g_low[t * 64 : t * 64 + 64, :] = low
        return g_high[...], g_low[...]

    moved = stack(jnp.where(inside, gradient, 0.0), 0)
    into = product(moved, image, NT)
    for t in range(9):
        for h in range(2):
            for j in range(2):
                out[pl.ds((t * 2 + h) * 2 + j, 32, stride=BACK), :] = into[
                    t * 64 + j * 32 : t * 64 + j * 32 + 32, h * 128 : h * 128 + 128
                ]
    shifts = [0, 1, STEP, STEP + 1]
    spread = jnp.concatenate([pltpu.roll(active, s, 1) if s else active for s in shifts], axis=0)
    onto = product(halves(spread), parts, NN)
    for t in range(9):
        at, kind = shifts.index(shift_of(t)) * 64, kind_of(t)
        for j in range(2):
            out[pl.ds(36 + t * 2 + j, 32, stride=BACK), :] = onto[
                at + j * 32 : at + j * 32 + 32, kind * 128 : kind * 128 + 128
            ]
    back = product(weights, stack(jnp.where(around, gradient, 0.0), -2 * STEP), TN)
    half = ROWS // 2 * STEP
    first = lax.axis_index("rows") % 2 == 0
    upper, lower = back[:, 0:256], pltpu.roll(back, FLAT - half, 1)[:, 0:256]
    for dst, part in (
        (mine, jnp.where(first, upper, lower)),
        (theirs, jnp.where(first, lower, upper)),
    ):
        for d in range(32):
            for q in range(2):
                dst[pl.ds(d * 16 + q * 8, 8), :] = part[d * 8 : d * 8 + 8, q * 128 : q * 128 + 128]
    blank = jnp.zeros((2, 128), F32)
    for d in range(32):
        out[pl.ds(d * BACK + 54, 2), :] = blank


def weights_kernel(scale, recv, mixed, total):
    mixed[...] = jnp.zeros_like(mixed)
    for core in range(2):
        each = recv[core]
        for block in range(1, 16):
            each = each + recv[2 * block + core]
        total[...] = each * scale
        for j in range(2):
            mixed[pl.ds(2 * core + j, 27, stride=4), :] = total[pl.ds(j, 27, stride=2), :]


def final_kernel(own, other, into, onto):
    first = lax.axis_index("rows") % 2 == 0
    sums = (
        jnp.where(first, own[...], other[...]),
        jnp.where(first, other[...], own[...]),
    )
    for k in range(27):
        tile = jnp.concatenate([x[4 * k : 4 * k + 4] for x in sums], axis=0)
        if k < 18:
            into[k // 2, :, (k % 2) * 128 : (k % 2) * 128 + 128] = tile
        else:
            onto[k - 18] = tile


def image_kernel(recv, out, image, line):
    image[...] = jnp.zeros_like(image)
    for block in range(16):
        start = 127 + BLOCK * block
        for q in range(2):
            at = slice(q * 8, q * 8 + 8)
            line[:, q * 128 : q * 128 + 128] = recv[2 * block, at, :] + recv[2 * block + 1, at, :]
        for r in range(ROWS // 2):
            image[r, :, start : start + STEP] += line[:, r * STEP : (r + 1) * STEP]
    for r in range(ROWS // 2):
        out[r] = image[r, :, 128:384]


def shape(*dims, dtype=F32):
    return jax.ShapeDtypeStruct(dims, dtype)


def call(kernel, outs, args, scratch=(), flops=10**6, moved=10**6, specs=None, grant=GRANT):
    return pl.pallas_call(
        kernel,
        out_shape=outs,
        in_specs=specs or [FULL] * args,
        out_specs=jax.tree.map(lambda _: FULL, outs),
        scratch_shapes=list(scratch),
        compiler_params=pltpu.CompilerParams(vmem_limit_bytes=grant),
        cost_estimate=pl.CostEstimate(flops=flops, bytes_accessed=moved, transcendentals=0),
    )


def partner(n):
    return [(i, i ^ 1) for i in range(n)]


def beside(n):
    return [(i, i + 1) for i in range(1, n - 1, 2)] + [(i, i - 1) for i in range(2, n, 2)]


def inward(n):
    return [(i, i + 2) for i in range(1, n - 2, 2)] + [(i, i - 2) for i in range(2, n, 2)]


def shifted(n, by):
    return [(i, (i + by) % n) for i in range(n)]


def local(features, weight_in, weight_out, cotangent):
    scale = (4.0 * features.shape[1] * lax.axis_size("rows") * features.shape[2]) ** (-0.5)
    flat = pltpu.VMEM((8, FLAT), F32)

    lines = jnp.transpose(features, (1, 0, 2))
    taps = jnp.transpose(weight_in, (1, 2, 0, 3)).reshape(9, 8, 256)
    edge, packed = call(
        prepare_kernel, (shape(80, 128), shape(32, PACK, 128)), 3,
        [
            pltpu.VMEM((2, 8, 256), F32), pltpu.VMEM((3, 16, 128), F32),
            pltpu.VMEM((9, 8, 256), F32), pltpu.VMEM((2, PACK, 128), F32),
            pltpu.SemaphoreType.DMA((3,)),
        ],
        specs=[pl.BlockSpec(memory_space=pltpu.HBM)] * 3, grant=MOST,
    )(lines, cotangent, taps)
    near = lax.ppermute(edge, "rows", beside(8))
    far = lax.ppermute(edge, "rows", inward(8))
    other = lax.ppermute(lines, "rows", partner(8))
    other_c = lax.ppermute(cotangent, "rows", partner(8))
    kernels = lax.all_to_all(packed, "chan", 0, 0, tiled=True)
    near, far, other, other_c, kernels = lax.optimization_barrier((near, far, other, other_c, kernels))
    packed = call(pack_kernel, shape(32, 32, 128), 4, [pltpu.VMEM((ROWS + 4, 8, 512), F32), flat])(
        lines, other, near, far
    )
    recv = lax.all_to_all(packed, "chan", 0, 0, tiled=True)

    tall, side = call(column_kernel, (shape(FINE, 16, 128), shape(FINE + 2, 128)), 4)(
        cotangent, other_c, near, far
    )
    near_side = lax.ppermute(side, "chan", beside(32))
    far_side = lax.ppermute(side, "chan", inward(32))
    other_tall = lax.ppermute(tall, "chan", partner(32))
    sent, own, given = call(
        main_kernel, (shape(32 * BACK, 128), shape(512, 128), shape(512, 128)), 7,
        [
            pltpu.VMEM((FINE, 48, 128), F32), pltpu.VMEM((FLAT, 512), F32),
            pltpu.VMEM((256, FLAT), BF16), pltpu.VMEM((256, FLAT), BF16),
            pltpu.VMEM((576, 256), BF16), pltpu.VMEM((576, 256), BF16),
            pltpu.VMEM((576, FLAT), BF16), pltpu.VMEM((576, FLAT), BF16),
        ],
        10**9, 5 * 10**6,
    )(
        recv.reshape(1024, 128), kernels.reshape(32 * PACK, 128), tall, other_tall, near_side, far_side,
        jnp.transpose(weight_out, (1, 2, 0, 3)).reshape(2304, 128),
    )
    given = lax.ppermute(given, "rows", partner(8))
    back = lax.all_to_all(sent.reshape(32, BACK, 128), "chan", 0, 0, tiled=True)
    moved, back = lax.optimization_barrier((own + given, back))
    mixed = call(lambda *refs: weights_kernel(scale, *refs), shape(112, 128), 1, [pltpu.VMEM((56, 128), F32)])(
        back
    )
    image = lax.all_to_all(moved.reshape(32, 16, 128), "chan", 0, 0, tiled=True)
    left = lax.ppermute(mixed, "rows", shifted(8, 2))
    right = lax.ppermute(mixed, "rows", shifted(8, 6))
    opposite = lax.ppermute(mixed, "rows", shifted(8, 4))
    mixed = (mixed + opposite) + (left + right)
    counter = lax.ppermute(mixed, "rows", partner(8))
    into, onto = call(final_kernel, (shape(9, 8, 256), shape(9, 8, 128)), 2)(mixed, counter)
    rows = call(
        image_kernel, shape(12, 8, 256), 1,
        [pltpu.VMEM((12, 8, 512), F32), pltpu.VMEM((8, 256), F32)], 10**11, 10**8,
    )(image)
    grad_image = jnp.transpose(rows, (1, 0, 2))
    grad_in = jnp.transpose(into.reshape(3, 3, 8, 256), (2, 0, 1, 3))
    grad_out = jnp.transpose(onto.reshape(3, 3, 8, 128), (2, 0, 1, 3))
    return (grad_image, grad_in, grad_out)


def solution(mesh):
    return jax.shard_map(
        local,
        mesh=mesh,
        in_specs=(
            P("chan", "rows", None),
            P("chan", None, None, None),
            P(),
            P("rows", "chan", None),
        ),
        out_specs=(
            P("chan", "rows", None),
            P("chan", None, None, None),
            P("chan", None, None, None),
        ),
        check_vma=False,
    )
```

```python
import jax
import jax.numpy as jnp
from jax import lax
from jax.experimental import pallas as pl
from jax.experimental.pallas import tpu as pltpu
from jax.sharding import PartitionSpec as P

BLOCK = 16
STEP = BLOCK + 2
ROWS = 24
FINE = 2 * ROWS + 6
FLAT = 512
PACK = 40
BACK = 56
F32, BF16 = jnp.float32, jnp.bfloat16
GRANT, MOST = 20 * 1024 * 1024, 60 * 1024 * 1024
FULL = pl.BlockSpec(memory_space=pltpu.VMEM)


def halves(x):
    high = x.astype(BF16)
    return high, (x - high.astype(F32)).astype(BF16)


def product(a, b, dims):
    def one(x, y):
        return lax.dot_general(x, y, (dims, ((), ())), preferred_element_type=F32)

    return one(a[0], b[0]) + (one(a[0], b[1]) + one(a[1], b[0]))


NN, NT, TN = ((1,), (0,)), ((1,), (1,)), ((0,), (0,))


def prepare_kernel(features, cotangent, weight, edge, packed, lines, cells, taps, part, sems):
    parity = lax.axis_index("rows") % 2
    half = ROWS // 2
    copies = [
        pltpu.make_async_copy(weight, taps, sems.at[0]),
        pltpu.make_async_copy(features.at[pl.ds((half - 2) * parity, 2)], lines, sems.at[1]),
        pltpu.make_async_copy(cotangent.at[pl.ds((ROWS - 3) * parity, 3)], cells, sems.at[2]),
    ]
    for copy in copies:
        copy.start()
    part[...] = jnp.zeros_like(part)
    for copy in copies:
        copy.wait()
    for k in range(2):
        for h in range(2):
            at = (2 * k + h) * 8
            edge[at : at + 8, :] = lines[k, :, h * 128 : h * 128 + 128]
    for k in range(3):
        edge[32 + k * 16 : 48 + k * 16, :] = cells[k]
    for t in range(9):
        rows = jnp.where(parity == 0, taps[t, 0:4, :], taps[t, 4:8, :])
        for core in range(2):
            for h in range(2):
                at = (t * 2 + h) * 2
                part[core, at : at + 2, :] = rows[
                    2 * core : 2 * core + 2, h * 128 : h * 128 + 128
                ]
    for core in range(2):
        tile = part[core]
        for block in range(16):
            packed[2 * block + core] = tile


def pack_kernel(own, other, near, far, out, image, line):
    parity = lax.axis_index("rows") % 2
    image[...] = jnp.zeros_like(image)
    line[...] = jnp.zeros_like(line)
    inner = slice(128, 384)
    half = ROWS // 2
    for i in range(half):
        image[2 + half * parity + i, :, inner] = own[i]
        image[2 + half * (1 - parity) + i, :, inner] = other[i]
    for edge, at in ((near, parity), (far, 1 - parity)):
        for k in range(2):
            for h in range(2):
                rows = (2 * k + h) * 8
                image[(ROWS + 2) * at + k, :, 128 + h * 128 : 256 + h * 128] = edge[rows : rows + 8]
    for block in range(16):
        start = 127 + BLOCK * block
        for r in range(ROWS + 4):
            line[:, r * STEP : (r + 1) * STEP] = image[r, :, start : start + STEP]
        for q in range(4):
            tile = line[:, q * 128 : (q + 1) * 128]
            out[2 * block, q * 8 : q * 8 + 8, :] = tile
            out[2 * block + 1, q * 8 : q * 8 + 8, :] = tile


def column_kernel(own, other, near, far, tall, side):
    parity = lax.axis_index("rows") % 2
    core = lax.axis_index("chan") % 2
    tall[pl.ds(3 + ROWS * parity, ROWS)] = own[...]
    tall[pl.ds(3 + ROWS * (1 - parity), ROWS)] = other[...]
    for edge, at in ((near, parity), (far, 1 - parity)):
        for k in range(3):
            tall[(2 * ROWS + 3) * at + k] = edge[32 + 16 * k : 48 + 16 * k]
    for r in range(FINE):
        line = tall[r]
        side[r : r + 1, :] = jnp.where(core == 0, line[0:1], line[15:16])
    side[FINE : FINE + 2, :] = jnp.zeros((2, 128), F32)


def windows(own, other, near, far, weight, sums, image):
    core = lax.axis_index("chan") % 2
    group = 2 * (lax.axis_index("rows") % 2) + core
    image[:, pl.ds(pl.multiple_of(8 + 16 * core, 8), 16), :] = own[...]
    image[:, pl.ds(pl.multiple_of(24 - 16 * core, 8), 16), :] = other[...]
    left = jnp.where(core == 0, near[...], far[...])
    right = jnp.where(core == 0, far[...], near[...])
    for r in range(FINE):
        image[r, 7:8, :] = left[r : r + 1]
        image[r, 40:41, :] = right[r : r + 1]
    sums[...] = jnp.zeros_like(sums)

    def cells(r, start, count):
        return image[r, pl.ds(start, count, stride=2), :]

    def pairs(r, start, count):
        return cells(r, start, count) + cells(r, start + 1, count)

    even = [pairs(r, 7, 17) for r in range(FINE)]
    odd = [pairs(r, 8, 16) for r in range(FINE)]
    for r in range(ROWS + 3):
        at = r * STEP
        sums[at : at + 17, 0:128] = even[2 * r] + even[2 * r + 1]
        sums[at : at + 16, 128:256] = odd[2 * r] + odd[2 * r + 1]
        if r < ROWS + 2:
            sums[at : at + 17, 256:384] = even[2 * r + 1] + even[2 * r + 2]
            sums[at : at + 16, 384:512] = odd[2 * r + 1] + odd[2 * r + 2]
    high, low = halves(sums[...])
    total = None
    for kind in range(4):
        lanes = slice(kind * 128, (kind + 1) * 128)
        taps = [t for t in range(9) if kind_of(t) == kind]
        left_side = jnp.concatenate(
            [
                weight[pl.ds(t * 256 + 2 * group + j, 32, stride=8), :]
                for t in taps
                for j in range(2)
            ],
            axis=0,
        )
        each = product(halves(left_side), (high[:, lanes], low[:, lanes]), NT)
        for i, t in enumerate(taps):
            term = each[i * 64 : (i + 1) * 64]
            if shift_of(t):
                term = pltpu.roll(term, FLAT - shift_of(t), 1)
            total = term if total is None else total + term
    return (high, low), total


def kind_of(t):
    return 2 * (t // 3 == 1) + (t % 3 == 1)


def shift_of(t):
    return STEP * (t // 3 == 0) + (t % 3 == 0)


def main_kernel(
    recv, kernels, own, other, near, far, weight, out, mine, theirs,
    cells, sums, x_high, x_low, w_high, w_low, g_high, g_low,
):
    parts, grad = windows(own, other, near, far, weight, sums, cells)
    for pair in range(16):
        for q in range(4):
            tile = jnp.concatenate(
                [recv[pl.ds((2 * pair + i) * 32 + q * 8, 8), :] for i in range(2)], axis=0
            )
            high, low = halves(tile)
            x_high[pair * 16 : pair * 16 + 16, q * 128 : q * 128 + 128] = high
            x_low[pair * 16 : pair * 16 + 16, q * 128 : q * 128 + 128] = low
    for t in range(9):
        for h in range(2):
            tile = jnp.concatenate(
                [kernels[pl.ds((t * 2 + h) * 2 + j, 32, stride=PACK), :] for j in range(2)], axis=0
            )
            high, low = halves(tile)
            w_high[t * 64 : t * 64 + 64, h * 128 : h * 128 + 128] = high
            w_low[t * 64 : t * 64 + 64, h * 128 : h * 128 + 128] = low
    weights = (w_high[...], w_low[...])
    image = (x_high[...], x_low[...])
    each = product(weights, image, NN)
    hidden = each[0:64]
    for t in range(1, 9):
        hidden = hidden + pltpu.roll(each[t * 64 : t * 64 + 64], FLAT - ((t // 3) * STEP + t % 3), 1)
    at = lax.broadcasted_iota(jnp.int32, (64, FLAT), 1)
    block = lax.axis_index("rows") // 2
    across = at % STEP < BLOCK
    inside = across & (at >= STEP) & (at < (ROWS + 1) * STEP)
    top = jnp.where(block == 0, STEP, 0)
    bottom = jnp.where(block == 3, (ROWS + 1) * STEP, (ROWS + 2) * STEP)
    around = across & (at >= top) & (at < bottom)
    sigma = 1.0 / (1.0 + jnp.exp(-hidden))
    active = jnp.where(inside, hidden * sigma, 0.0)
    slope = sigma * (1.0 + hidden * (1.0 - sigma))
    gradient = grad * slope

    def stack(values, offset):
        for t in range(9):
            shift = ((t // 3) * STEP + t % 3 + offset) % FLAT
            high, low = halves(pltpu.roll(values, shift, 1) if shift else values)
            g_high[t * 64 : t * 64 + 64, :] = high
            g_low[t * 64 : t * 64 + 64, :] = low
        return g_high[...], g_low[...]

    moved = stack(jnp.where(inside, gradient, 0.0), 0)
    into = product(moved, image, NT)
    for t in range(9):
        for h in range(2):
            for j in range(2):
                out[pl.ds((t * 2 + h) * 2 + j, 32, stride=BACK), :] = into[
                    t * 64 + j * 32 : t * 64 + j * 32 + 32, h * 128 : h * 128 + 128
                ]
    shifts = [0, 1, STEP, STEP + 1]
    spread = jnp.concatenate([pltpu.roll(active, s, 1) if s else active for s in shifts], axis=0)
    onto = product(halves(spread), parts, NN)
    for t in range(9):
        at, kind = shifts.index(shift_of(t)) * 64, kind_of(t)
        for j in range(2):
            out[pl.ds(36 + t * 2 + j, 32, stride=BACK), :] = onto[
                at + j * 32 : at + j * 32 + 32, kind * 128 : kind * 128 + 128
            ]
    back = product(weights, stack(jnp.where(around, gradient, 0.0), -2 * STEP), TN)
    half = ROWS // 2 * STEP
    first = lax.axis_index("rows") % 2 == 0
    upper, lower = back[:, 0:256], pltpu.roll(back, FLAT - half, 1)[:, 0:256]
    for dst, part in (
        (mine, jnp.where(first, upper, lower)),
        (theirs, jnp.where(first, lower, upper)),
    ):
        for d in range(32):
            for q in range(2):
                dst[pl.ds(d * 16 + q * 8, 8), :] = part[d * 8 : d * 8 + 8, q * 128 : q * 128 + 128]
    blank = jnp.zeros((2, 128), F32)
    for d in range(32):
        out[pl.ds(d * BACK + 54, 2), :] = blank


def weights_kernel(scale, recv, mixed, total):
    mixed[...] = jnp.zeros_like(mixed)
    for core in range(2):
        each = recv[core]
        for block in range(1, 16):
            each = each + recv[2 * block + core]
        total[...] = each * scale
        for j in range(2):
            mixed[pl.ds(2 * core + j, 27, stride=4), :] = total[pl.ds(j, 27, stride=2), :]


def add_kernel(own, other, total):
    total[...] = own[...] + other[...]


def final_kernel(own, other, into, onto):
    first = lax.axis_index("rows") % 2 == 0
    sums = (
        jnp.where(first, own[...], other[...]),
        jnp.where(first, other[...], own[...]),
    )
    for k in range(27):
        tile = jnp.concatenate([x[4 * k : 4 * k + 4] for x in sums], axis=0)
        if k < 18:
            into[k // 2, :, (k % 2) * 128 : (k % 2) * 128 + 128] = tile
        else:
            onto[k - 18] = tile


def image_kernel(recv, out, image, line):
    image[...] = jnp.zeros_like(image)
    for block in range(16):
        start = 127 + BLOCK * block
        for q in range(2):
            at = slice(q * 8, q * 8 + 8)
            line[:, q * 128 : q * 128 + 128] = recv[2 * block, at, :] + recv[2 * block + 1, at, :]
        for r in range(ROWS // 2):
            image[r, :, start : start + STEP] += line[:, r * STEP : (r + 1) * STEP]
    for r in range(ROWS // 2):
        out[r] = image[r, :, 128:384]


def shape(*dims, dtype=F32):
    return jax.ShapeDtypeStruct(dims, dtype)


def call(kernel, outs, args, scratch=(), flops=10**6, moved=10**6, specs=None, grant=GRANT):
    return pl.pallas_call(
        kernel,
        out_shape=outs,
        in_specs=specs or [FULL] * args,
        out_specs=jax.tree.map(lambda _: FULL, outs),
        scratch_shapes=list(scratch),
        compiler_params=pltpu.CompilerParams(vmem_limit_bytes=grant),
        cost_estimate=pl.CostEstimate(flops=flops, bytes_accessed=moved, transcendentals=0),
    )


def partner(n, by=1):
    return [(i, i ^ by) for i in range(n)]


def beside(n):
    return [(i, i + 1) for i in range(1, n - 1, 2)] + [(i, i - 1) for i in range(2, n, 2)]


def inward(n):
    return [(i, i + 2) for i in range(1, n - 2, 2)] + [(i, i - 2) for i in range(2, n, 2)]


def mirrored(n):
    return [(i, (n - 2 - i + 2 * (i % 2)) % n) for i in range(n)]


def local(features, weight_in, weight_out, cotangent):
    scale = (4.0 * features.shape[1] * lax.axis_size("rows") * features.shape[2]) ** (-0.5)
    flat = pltpu.VMEM((8, FLAT), F32)

    lines = jnp.transpose(features, (1, 0, 2))
    taps = jnp.transpose(weight_in, (1, 2, 0, 3)).reshape(9, 8, 256)
    edge, packed = call(
        prepare_kernel, (shape(80, 128), shape(32, PACK, 128)), 3,
        [
            pltpu.VMEM((2, 8, 256), F32), pltpu.VMEM((3, 16, 128), F32),
            pltpu.VMEM((9, 8, 256), F32), pltpu.VMEM((2, PACK, 128), F32),
            pltpu.SemaphoreType.DMA((3,)),
        ],
        specs=[pl.BlockSpec(memory_space=pltpu.HBM)] * 3, grant=MOST,
    )(lines, cotangent, taps)
    near = lax.ppermute(edge, "rows", beside(8))
    far = lax.ppermute(edge, "rows", inward(8))
    other = lax.ppermute(lines, "rows", partner(8))
    other_c = lax.ppermute(cotangent, "rows", partner(8))
    kernels = lax.all_to_all(packed, "chan", 0, 0, tiled=True)
    near, far, other, other_c, kernels = lax.optimization_barrier((near, far, other, other_c, kernels))
    packed = call(pack_kernel, shape(32, 32, 128), 4, [pltpu.VMEM((ROWS + 4, 8, 512), F32), flat])(
        lines, other, near, far
    )
    recv = lax.all_to_all(packed, "chan", 0, 0, tiled=True)

    tall, side = call(column_kernel, (shape(FINE, 16, 128), shape(FINE + 2, 128)), 4)(
        cotangent, other_c, near, far
    )
    near_side = lax.ppermute(side, "chan", beside(32))
    other_tall = lax.ppermute(tall, "chan", partner(32))
    far_side = lax.ppermute(near_side, "chan", partner(32))
    sent, own, given = call(
        main_kernel, (shape(32 * BACK, 128), shape(512, 128), shape(512, 128)), 7,
        [
            pltpu.VMEM((FINE, 48, 128), F32), pltpu.VMEM((FLAT, 512), F32),
            pltpu.VMEM((256, FLAT), BF16), pltpu.VMEM((256, FLAT), BF16),
            pltpu.VMEM((576, 256), BF16), pltpu.VMEM((576, 256), BF16),
            pltpu.VMEM((576, FLAT), BF16), pltpu.VMEM((576, FLAT), BF16),
        ],
        10**9, 5 * 10**6,
    )(
        recv.reshape(1024, 128), kernels.reshape(32 * PACK, 128), tall, other_tall, near_side, far_side,
        jnp.transpose(weight_out, (1, 2, 0, 3)).reshape(2304, 128),
    )
    given = lax.ppermute(given, "rows", partner(8))
    back = lax.all_to_all(sent.reshape(32, BACK, 128), "chan", 0, 0, tiled=True)
    moved, back = lax.optimization_barrier((own + given, back))
    mixed = call(lambda *refs: weights_kernel(scale, *refs), shape(112, 128), 1, [pltpu.VMEM((56, 128), F32)])(
        back
    )
    moved, mixed = lax.optimization_barrier((moved, mixed))
    image = lax.all_to_all(moved.reshape(32, 16, 128), "chan", 0, 0, tiled=True)
    opposite = lax.ppermute(mixed, "rows", partner(8, 2))
    mixed = call(add_kernel, shape(112, 128), 2, (), 10**10, 10**7)(mixed, opposite)
    opposite = lax.ppermute(mixed, "rows", mirrored(8))
    mixed = mixed + opposite
    counter = lax.ppermute(mixed, "rows", partner(8))
    into, onto = call(final_kernel, (shape(9, 8, 256), shape(9, 8, 128)), 2)(mixed, counter)
    rows = call(
        image_kernel, shape(12, 8, 256), 1,
        [pltpu.VMEM((12, 8, 512), F32), pltpu.VMEM((8, 256), F32)], 10**11, 10**8,
    )(image)
    grad_image = jnp.transpose(rows, (1, 0, 2))
    grad_in = jnp.transpose(into.reshape(3, 3, 8, 256), (2, 0, 1, 3))
    grad_out = jnp.transpose(onto.reshape(3, 3, 8, 128), (2, 0, 1, 3))
    return (grad_image, grad_in, grad_out)


def solution(mesh):
    return jax.shard_map(
        local,
        mesh=mesh,
        in_specs=(
            P("chan", "rows", None),
            P("chan", None, None, None),
            P(),
            P("rows", "chan", None),
        ),
        out_specs=(
            P("chan", "rows", None),
            P("chan", None, None, None),
            P("chan", None, None, None),
        ),
        check_vma=False,
    )
```

```python
import jax
import jax.numpy as jnp
from jax import lax
from jax.experimental import pallas as pl
from jax.experimental.pallas import tpu as pltpu
from jax.sharding import PartitionSpec as P

BLOCK = 16
STEP = BLOCK + 2
ROWS = 24
FINE = 2 * ROWS + 6
FLAT = 512
PACK = 40
BACK = 56
F32, BF16 = jnp.float32, jnp.bfloat16
GRANT, MOST = 20 * 1024 * 1024, 60 * 1024 * 1024
FULL = pl.BlockSpec(memory_space=pltpu.VMEM)


def halves(x):
    high = x.astype(BF16)
    return high, (x - high.astype(F32)).astype(BF16)


def product(a, b, dims):
    def one(x, y):
        return lax.dot_general(x, y, (dims, ((), ())), preferred_element_type=F32)

    return one(a[0], b[0]) + (one(a[0], b[1]) + one(a[1], b[0]))


NN, NT, TN = ((1,), (0,)), ((1,), (1,)), ((0,), (0,))


def prepare_kernel(features, cotangent, weight, edge, packed, lines, cells, taps, part, sems):
    parity = lax.axis_index("rows") % 2
    half = ROWS // 2
    copies = [
        pltpu.make_async_copy(weight, taps, sems.at[0]),
        pltpu.make_async_copy(features.at[pl.ds((half - 2) * parity, 2)], lines, sems.at[1]),
        pltpu.make_async_copy(cotangent.at[pl.ds((ROWS - 3) * parity, 3)], cells, sems.at[2]),
    ]
    for copy in copies:
        copy.start()
    part[...] = jnp.zeros_like(part)
    for copy in copies:
        copy.wait()
    for k in range(2):
        for h in range(2):
            at = (2 * k + h) * 8
            edge[at : at + 8, :] = lines[k, :, h * 128 : h * 128 + 128]
    for k in range(3):
        edge[32 + k * 16 : 48 + k * 16, :] = cells[k]
    for t in range(9):
        rows = jnp.where(parity == 0, taps[t, 0:4, :], taps[t, 4:8, :])
        for core in range(2):
            for h in range(2):
                at = (t * 2 + h) * 2
                part[core, at : at + 2, :] = rows[
                    2 * core : 2 * core + 2, h * 128 : h * 128 + 128
                ]
    for core in range(2):
        tile = part[core]
        for block in range(16):
            packed[2 * block + core] = tile


def pack_kernel(own, other, near, far, out, image, line):
    parity = lax.axis_index("rows") % 2
    image[...] = jnp.zeros_like(image)
    line[...] = jnp.zeros_like(line)
    inner = slice(128, 384)
    half = ROWS // 2
    for i in range(half):
        image[2 + half * parity + i, :, inner] = own[i]
        image[2 + half * (1 - parity) + i, :, inner] = other[i]
    for edge, at in ((near, parity), (far, 1 - parity)):
        for k in range(2):
            for h in range(2):
                rows = (2 * k + h) * 8
                image[(ROWS + 2) * at + k, :, 128 + h * 128 : 256 + h * 128] = edge[rows : rows + 8]
    for block in range(16):
        start = 127 + BLOCK * block
        for r in range(ROWS + 4):
            line[:, r * STEP : (r + 1) * STEP] = image[r, :, start : start + STEP]
        for q in range(4):
            tile = line[:, q * 128 : (q + 1) * 128]
            out[2 * block, q * 8 : q * 8 + 8, :] = tile
            out[2 * block + 1, q * 8 : q * 8 + 8, :] = tile


def column_kernel(own, other, near, far, tall, side):
    parity = lax.axis_index("rows") % 2
    core = lax.axis_index("chan") % 2
    tall[pl.ds(3 + ROWS * parity, ROWS)] = own[...]
    tall[pl.ds(3 + ROWS * (1 - parity), ROWS)] = other[...]
    for edge, at in ((near, parity), (far, 1 - parity)):
        for k in range(3):
            tall[(2 * ROWS + 3) * at + k] = edge[32 + 16 * k : 48 + 16 * k]
    for r in range(FINE):
        line = tall[r]
        side[r : r + 1, :] = jnp.where(core == 0, line[0:1], line[15:16])
    side[FINE : FINE + 2, :] = jnp.zeros((2, 128), F32)


def windows(own, other, near, far, weight, sums, image):
    core = lax.axis_index("chan") % 2
    group = 2 * (lax.axis_index("rows") % 2) + core
    image[:, pl.ds(pl.multiple_of(8 + 16 * core, 8), 16), :] = own[...]
    image[:, pl.ds(pl.multiple_of(24 - 16 * core, 8), 16), :] = other[...]
    left = jnp.where(core == 0, near[...], far[...])
    right = jnp.where(core == 0, far[...], near[...])
    for r in range(FINE):
        image[r, 7:8, :] = left[r : r + 1]
        image[r, 40:41, :] = right[r : r + 1]
    sums[...] = jnp.zeros_like(sums)

    def cells(r, start, count):
        return image[r, pl.ds(start, count, stride=2), :]

    def pairs(r, start, count):
        return cells(r, start, count) + cells(r, start + 1, count)

    even = [pairs(r, 7, 17) for r in range(FINE)]
    odd = [pairs(r, 8, 16) for r in range(FINE)]
    for r in range(ROWS + 3):
        at = r * STEP
        sums[at : at + 17, 0:128] = even[2 * r] + even[2 * r + 1]
        sums[at : at + 16, 128:256] = odd[2 * r] + odd[2 * r + 1]
        if r < ROWS + 2:
            sums[at : at + 17, 256:384] = even[2 * r + 1] + even[2 * r + 2]
            sums[at : at + 16, 384:512] = odd[2 * r + 1] + odd[2 * r + 2]
    high, low = halves(sums[...])
    total = None
    for kind in range(4):
        lanes = slice(kind * 128, (kind + 1) * 128)
        taps = [t for t in range(9) if kind_of(t) == kind]
        left_side = jnp.concatenate(
            [
                weight[pl.ds(t * 256 + 2 * group + j, 32, stride=8), :]
                for t in taps
                for j in range(2)
            ],
            axis=0,
        )
        each = product(halves(left_side), (high[:, lanes], low[:, lanes]), NT)
        for i, t in enumerate(taps):
            term = each[i * 64 : (i + 1) * 64]
            if shift_of(t):
                term = pltpu.roll(term, FLAT - shift_of(t), 1)
            total = term if total is None else total + term
    return (high, low), total


def kind_of(t):
    return 2 * (t // 3 == 1) + (t % 3 == 1)


def shift_of(t):
    return STEP * (t // 3 == 0) + (t % 3 == 0)


def main_kernel(
    recv, kernels, own, other, near, far, weight, out, mine, theirs,
    cells, sums, x_high, x_low, w_high, w_low, g_high, g_low,
):
    parts, grad = windows(own, other, near, far, weight, sums, cells)
    for pair in range(16):
        for q in range(4):
            tile = jnp.concatenate(
                [recv[pl.ds((2 * pair + i) * 32 + q * 8, 8), :] for i in range(2)], axis=0
            )
            high, low = halves(tile)
            x_high[pair * 16 : pair * 16 + 16, q * 128 : q * 128 + 128] = high
            x_low[pair * 16 : pair * 16 + 16, q * 128 : q * 128 + 128] = low
    for t in range(9):
        for h in range(2):
            tile = jnp.concatenate(
                [kernels[pl.ds((t * 2 + h) * 2 + j, 32, stride=PACK), :] for j in range(2)], axis=0
            )
            high, low = halves(tile)
            w_high[t * 64 : t * 64 + 64, h * 128 : h * 128 + 128] = high
            w_low[t * 64 : t * 64 + 64, h * 128 : h * 128 + 128] = low
    weights = (w_high[...], w_low[...])
    image = (x_high[...], x_low[...])
    each = product(weights, image, NN)
    hidden = each[0:64]
    for t in range(1, 9):
        hidden = hidden + pltpu.roll(each[t * 64 : t * 64 + 64], FLAT - ((t // 3) * STEP + t % 3), 1)
    at = lax.broadcasted_iota(jnp.int32, (64, FLAT), 1)
    block = lax.axis_index("rows") // 2
    across = at % STEP < BLOCK
    inside = across & (at >= STEP) & (at < (ROWS + 1) * STEP)
    top = jnp.where(block == 0, STEP, 0)
    bottom = jnp.where(block == 3, (ROWS + 1) * STEP, (ROWS + 2) * STEP)
    around = across & (at >= top) & (at < bottom)
    sigma = 1.0 / (1.0 + jnp.exp(-hidden))
    active = jnp.where(inside, hidden * sigma, 0.0)
    slope = sigma * (1.0 + hidden * (1.0 - sigma))
    gradient = grad * slope

    def stack(values, offset):
        for t in range(9):
            shift = ((t // 3) * STEP + t % 3 + offset) % FLAT
            high, low = halves(pltpu.roll(values, shift, 1) if shift else values)
            g_high[t * 64 : t * 64 + 64, :] = high
            g_low[t * 64 : t * 64 + 64, :] = low
        return g_high[...], g_low[...]

    moved = stack(jnp.where(inside, gradient, 0.0), 0)
    into = product(moved, image, NT)
    for t in range(9):
        for h in range(2):
            for j in range(2):
                out[pl.ds((t * 2 + h) * 2 + j, 32, stride=BACK), :] = into[
                    t * 64 + j * 32 : t * 64 + j * 32 + 32, h * 128 : h * 128 + 128
                ]
    shifts = [0, 1, STEP, STEP + 1]
    spread = jnp.concatenate([pltpu.roll(active, s, 1) if s else active for s in shifts], axis=0)
    onto = product(halves(spread), parts, NN)
    for t in range(9):
        at, kind = shifts.index(shift_of(t)) * 64, kind_of(t)
        for j in range(2):
            out[pl.ds(36 + t * 2 + j, 32, stride=BACK), :] = onto[
                at + j * 32 : at + j * 32 + 32, kind * 128 : kind * 128 + 128
            ]
    back = product(weights, stack(jnp.where(around, gradient, 0.0), -2 * STEP), TN)
    half = ROWS // 2 * STEP
    first = lax.axis_index("rows") % 2 == 0
    upper, lower = back[:, 0:256], pltpu.roll(back, FLAT - half, 1)[:, 0:256]
    for dst, part in (
        (mine, jnp.where(first, upper, lower)),
        (theirs, jnp.where(first, lower, upper)),
    ):
        for d in range(32):
            for q in range(2):
                dst[pl.ds(d * 16 + q * 8, 8), :] = part[d * 8 : d * 8 + 8, q * 128 : q * 128 + 128]
    blank = jnp.zeros((2, 128), F32)
    for d in range(32):
        out[pl.ds(d * BACK + 54, 2), :] = blank


def weights_kernel(scale, recv, mixed, total):
    mixed[...] = jnp.zeros_like(mixed)
    for core in range(2):
        each = recv[core]
        for block in range(1, 16):
            each = each + recv[2 * block + core]
        total[...] = each * scale
        for j in range(2):
            mixed[pl.ds(2 * core + j, 27, stride=4), :] = total[pl.ds(j, 27, stride=2), :]


def add_kernel(own, other, total):
    total[...] = own[...] + other[...]


def final_kernel(own, other, into, onto):
    first = lax.axis_index("rows") % 2 == 0
    sums = (
        jnp.where(first, own[...], other[...]),
        jnp.where(first, other[...], own[...]),
    )
    for k in range(27):
        tile = jnp.concatenate([x[4 * k : 4 * k + 4] for x in sums], axis=0)
        if k < 18:
            into[k // 2, :, (k % 2) * 128 : (k % 2) * 128 + 128] = tile
        else:
            onto[k - 18] = tile


def image_kernel(recv, out, image, line):
    image[...] = jnp.zeros_like(image)
    for block in range(16):
        start = 127 + BLOCK * block
        for q in range(2):
            at = slice(q * 8, q * 8 + 8)
            line[:, q * 128 : q * 128 + 128] = recv[2 * block, at, :] + recv[2 * block + 1, at, :]
        for r in range(ROWS // 2):
            image[r, :, start : start + STEP] += line[:, r * STEP : (r + 1) * STEP]
    for r in range(ROWS // 2):
        out[r] = image[r, :, 128:384]


def shape(*dims, dtype=F32):
    return jax.ShapeDtypeStruct(dims, dtype)


def call(kernel, outs, args, scratch=(), flops=10**6, moved=10**6, specs=None, grant=GRANT):
    return pl.pallas_call(
        kernel,
        out_shape=outs,
        in_specs=specs or [FULL] * args,
        out_specs=jax.tree.map(lambda _: FULL, outs),
        scratch_shapes=list(scratch),
        compiler_params=pltpu.CompilerParams(vmem_limit_bytes=grant),
        cost_estimate=pl.CostEstimate(flops=flops, bytes_accessed=moved, transcendentals=0),
    )


def partner(n, by=1):
    return [(i, i ^ by) for i in range(n)]


def beside(n):
    return [(i, i + 1) for i in range(1, n - 1, 2)] + [(i, i - 1) for i in range(2, n, 2)]


def inward(n):
    return [(i, i + 2) for i in range(1, n - 2, 2)] + [(i, i - 2) for i in range(2, n, 2)]


def mirrored(n):
    return [(i, (n - 2 - i + 2 * (i % 2)) % n) for i in range(n)]


def local(features, weight_in, weight_out, cotangent):
    scale = (4.0 * features.shape[1] * lax.axis_size("rows") * features.shape[2]) ** (-0.5)
    flat = pltpu.VMEM((8, FLAT), F32)

    lines = jnp.transpose(features, (1, 0, 2))
    taps = jnp.transpose(weight_in, (1, 2, 0, 3)).reshape(9, 8, 256)
    edge, packed = call(
        prepare_kernel, (shape(80, 128), shape(32, PACK, 128)), 3,
        [
            pltpu.VMEM((2, 8, 256), F32), pltpu.VMEM((3, 16, 128), F32),
            pltpu.VMEM((9, 8, 256), F32), pltpu.VMEM((2, PACK, 128), F32),
            pltpu.SemaphoreType.DMA((3,)),
        ],
        specs=[pl.BlockSpec(memory_space=pltpu.HBM)] * 3, grant=MOST,
    )(lines, cotangent, taps)
    near = lax.ppermute(edge, "rows", beside(8))
    far = lax.ppermute(edge, "rows", inward(8))
    other = lax.ppermute(lines, "rows", partner(8))
    other_c = lax.ppermute(cotangent, "rows", partner(8))
    kernels = lax.all_to_all(packed, "chan", 0, 0, tiled=True)
    near, far, other, other_c, kernels = lax.optimization_barrier((near, far, other, other_c, kernels))
    packed = call(pack_kernel, shape(32, 32, 128), 4, [pltpu.VMEM((ROWS + 4, 8, 512), F32), flat])(
        lines, other, near, far
    )
    recv = lax.all_to_all(packed, "chan", 0, 0, tiled=True)

    tall, side = call(column_kernel, (shape(FINE, 16, 128), shape(FINE + 2, 128)), 4)(
        cotangent, other_c, near, far
    )
    near_side = lax.ppermute(side, "chan", beside(32))
    other_tall = lax.ppermute(tall, "chan", partner(32))
    far_side = lax.ppermute(near_side, "chan", partner(32))
    sent, own, given = call(
        main_kernel, (shape(32 * BACK, 128), shape(512, 128), shape(512, 128)), 7,
        [
            pltpu.VMEM((FINE, 48, 128), F32), pltpu.VMEM((FLAT, 512), F32),
            pltpu.VMEM((256, FLAT), BF16), pltpu.VMEM((256, FLAT), BF16),
            pltpu.VMEM((576, 256), BF16), pltpu.VMEM((576, 256), BF16),
            pltpu.VMEM((576, FLAT), BF16), pltpu.VMEM((576, FLAT), BF16),
        ],
        10**9, 5 * 10**6,
    )(
        recv.reshape(1024, 128), kernels.reshape(32 * PACK, 128), tall, other_tall, near_side, far_side,
        jnp.transpose(weight_out, (1, 2, 0, 3)).reshape(2304, 128),
    )
    given = lax.ppermute(given, "rows", partner(8))
    back = lax.all_to_all(sent.reshape(32, BACK, 128), "chan", 0, 0, tiled=True)
    moved, back = lax.optimization_barrier((own + given, back))
    mixed = call(lambda *refs: weights_kernel(scale, *refs), shape(112, 128), 1, [pltpu.VMEM((56, 128), F32)])(
        back
    )
    moved, mixed = lax.optimization_barrier((moved, mixed))
    image = lax.all_to_all(moved.reshape(32, 16, 128), "chan", 0, 0, tiled=True)
    opposite = lax.ppermute(mixed, "rows", partner(8, 2))
    mixed = call(add_kernel, shape(112, 128), 2, (), 10**10, 10**7)(mixed, opposite)
    opposite = lax.ppermute(mixed, "rows", mirrored(8))
    mixed = mixed + opposite
    counter = lax.ppermute(mixed, "rows", partner(8))
    rows = call(
        image_kernel, shape(12, 8, 256), 1,
        [pltpu.VMEM((12, 8, 512), F32), pltpu.VMEM((8, 256), F32)],
    )(image)
    rows, counter = lax.optimization_barrier((rows, counter))
    into, onto = call(final_kernel, (shape(9, 8, 256), shape(9, 8, 128)), 2)(mixed, counter)
    grad_image = jnp.transpose(rows, (1, 0, 2))
    grad_in = jnp.transpose(into.reshape(3, 3, 8, 256), (2, 0, 1, 3))
    grad_out = jnp.transpose(onto.reshape(3, 3, 8, 128), (2, 0, 1, 3))
    return (grad_image, grad_in, grad_out)


def solution(mesh):
    return jax.shard_map(
        local,
        mesh=mesh,
        in_specs=(
            P("chan", "rows", None),
            P("chan", None, None, None),
            P(),
            P("rows", "chan", None),
        ),
        out_specs=(
            P("chan", "rows", None),
            P("chan", None, None, None),
            P("chan", None, None, None),
        ),
        check_vma=False,
    )
```

```python
import jax
import jax.numpy as jnp
from jax import lax
from jax.experimental import pallas as pl
from jax.experimental.pallas import tpu as pltpu
from jax.sharding import PartitionSpec as P

BLOCK = 16
STEP = BLOCK + 2
ROWS = 24
FINE = 2 * ROWS + 6
FLAT = 512
PACK = 40
BACK = 56
F32, BF16 = jnp.float32, jnp.bfloat16
GRANT, MOST = 20 * 1024 * 1024, 60 * 1024 * 1024
FULL = pl.BlockSpec(memory_space=pltpu.VMEM)


def halves(x):
    high = x.astype(BF16)
    return high, (x - high.astype(F32)).astype(BF16)


def product(a, b, dims):
    def one(x, y):
        return lax.dot_general(x, y, (dims, ((), ())), preferred_element_type=F32)

    return one(a[0], b[0]) + (one(a[0], b[1]) + one(a[1], b[0]))


NN, NT, TN = ((1,), (0,)), ((1,), (1,)), ((0,), (0,))


def prepare_kernel(features, cotangent, weight, edge, packed, lines, cells, taps, part, sems):
    parity = lax.axis_index("rows") % 2
    half = ROWS // 2
    copies = [
        pltpu.make_async_copy(weight, taps, sems.at[0]),
        pltpu.make_async_copy(features.at[pl.ds((half - 2) * parity, 2)], lines, sems.at[1]),
        pltpu.make_async_copy(cotangent.at[pl.ds((ROWS - 3) * parity, 3)], cells, sems.at[2]),
    ]
    for copy in copies:
        copy.start()
    part[...] = jnp.zeros_like(part)
    for copy in copies:
        copy.wait()
    for k in range(2):
        for h in range(2):
            at = (2 * k + h) * 8
            edge[at : at + 8, :] = lines[k, :, h * 128 : h * 128 + 128]
    for k in range(3):
        edge[32 + k * 16 : 48 + k * 16, :] = cells[k]
    for t in range(9):
        rows = jnp.where(parity == 0, taps[t, 0:4, :], taps[t, 4:8, :])
        for core in range(2):
            for h in range(2):
                at = (t * 2 + h) * 2
                part[core, at : at + 2, :] = rows[
                    2 * core : 2 * core + 2, h * 128 : h * 128 + 128
                ]
    for core in range(2):
        tile = part[core]
        for block in range(16):
            packed[2 * block + core] = tile


def pack_kernel(own, other, near, far, out, image, line):
    parity = lax.axis_index("rows") % 2
    image[...] = jnp.zeros_like(image)
    line[...] = jnp.zeros_like(line)
    inner = slice(128, 384)
    half = ROWS // 2
    for i in range(half):
        image[2 + half * parity + i, :, inner] = own[i]
        image[2 + half * (1 - parity) + i, :, inner] = other[i]
    for edge, at in ((near, parity), (far, 1 - parity)):
        for k in range(2):
            for h in range(2):
                rows = (2 * k + h) * 8
                image[(ROWS + 2) * at + k, :, 128 + h * 128 : 256 + h * 128] = edge[rows : rows + 8]
    for block in range(16):
        start = 127 + BLOCK * block
        for r in range(ROWS + 4):
            line[:, r * STEP : (r + 1) * STEP] = image[r, :, start : start + STEP]
        for q in range(4):
            tile = line[:, q * 128 : (q + 1) * 128]
            out[2 * block, q * 8 : q * 8 + 8, :] = tile
            out[2 * block + 1, q * 8 : q * 8 + 8, :] = tile


def column_kernel(own, other, near, far, tall, side):
    parity = lax.axis_index("rows") % 2
    core = lax.axis_index("chan") % 2
    tall[pl.ds(3 + ROWS * parity, ROWS)] = own[...]
    tall[pl.ds(3 + ROWS * (1 - parity), ROWS)] = other[...]
    for edge, at in ((near, parity), (far, 1 - parity)):
        for k in range(3):
            tall[(2 * ROWS + 3) * at + k] = edge[32 + 16 * k : 48 + 16 * k]
    for r in range(FINE):
        line = tall[r]
        side[r : r + 1, :] = jnp.where(core == 0, line[0:1], line[15:16])
    side[FINE : FINE + 2, :] = jnp.zeros((2, 128), F32)


def windows(own, other, near, far, weight, sums, image):
    core = lax.axis_index("chan") % 2
    group = 2 * (lax.axis_index("rows") % 2) + core
    image[:, pl.ds(pl.multiple_of(8 + 16 * core, 8), 16), :] = own[...]
    image[:, pl.ds(pl.multiple_of(24 - 16 * core, 8), 16), :] = other[...]
    left = jnp.where(core == 0, near[...], far[...])
    right = jnp.where(core == 0, far[...], near[...])
    for r in range(FINE):
        image[r, 7:8, :] = left[r : r + 1]
        image[r, 40:41, :] = right[r : r + 1]
    sums[...] = jnp.zeros_like(sums)

    def cells(r, start, count):
        return image[r, pl.ds(start, count, stride=2), :]

    def pairs(r, start, count):
        return cells(r, start, count) + cells(r, start + 1, count)

    even = [pairs(r, 7, 17) for r in range(FINE)]
    odd = [pairs(r, 8, 16) for r in range(FINE)]
    for r in range(ROWS + 3):
        at = r * STEP
        sums[at : at + 17, 0:128] = even[2 * r] + even[2 * r + 1]
        sums[at : at + 16, 128:256] = odd[2 * r] + odd[2 * r + 1]
        if r < ROWS + 2:
            sums[at : at + 17, 256:384] = even[2 * r + 1] + even[2 * r + 2]
            sums[at : at + 16, 384:512] = odd[2 * r + 1] + odd[2 * r + 2]
    high, low = halves(sums[...])
    total = None
    for kind in range(4):
        lanes = slice(kind * 128, (kind + 1) * 128)
        taps = [t for t in range(9) if kind_of(t) == kind]
        left_side = jnp.concatenate(
            [
                weight[pl.ds(t * 256 + 2 * group + j, 32, stride=8), :]
                for t in taps
                for j in range(2)
            ],
            axis=0,
        )
        each = product(halves(left_side), (high[:, lanes], low[:, lanes]), NT)
        for i, t in enumerate(taps):
            term = each[i * 64 : (i + 1) * 64]
            if shift_of(t):
                term = pltpu.roll(term, FLAT - shift_of(t), 1)
            total = term if total is None else total + term
    return (high, low), total


def kind_of(t):
    return 2 * (t // 3 == 1) + (t % 3 == 1)


def shift_of(t):
    return STEP * (t // 3 == 0) + (t % 3 == 0)


def hidden_kernel(recv, kernels, result, x_high, x_low, w_high, w_low):
    for pair in range(16):
        for q in range(4):
            tile = jnp.concatenate(
                [recv[pl.ds((2 * pair + i) * 32 + q * 8, 8), :] for i in range(2)], axis=0
            )
            high, low = halves(tile)
            x_high[pair * 16 : pair * 16 + 16, q * 128 : q * 128 + 128] = high
            x_low[pair * 16 : pair * 16 + 16, q * 128 : q * 128 + 128] = low
    for t in range(9):
        for h in range(2):
            tile = jnp.concatenate(
                [kernels[pl.ds((t * 2 + h) * 2 + j, 32, stride=PACK), :] for j in range(2)], axis=0
            )
            high, low = halves(tile)
            w_high[t * 64 : t * 64 + 64, h * 128 : h * 128 + 128] = high
            w_low[t * 64 : t * 64 + 64, h * 128 : h * 128 + 128] = low
    weights = (w_high[...], w_low[...])
    image = (x_high[...], x_low[...])
    each = product(weights, image, NN)
    hidden = each[0:64]
    for t in range(1, 9):
        hidden = hidden + pltpu.roll(each[t * 64 : t * 64 + 64], FLAT - ((t // 3) * STEP + t % 3), 1)
    result[...] = hidden


def main_kernel(
    forward, x_high, x_low, w_high, w_low, own, other, near, far, weight, out, mine, theirs,
    cells, sums, g_high, g_low,
):
    parts, grad = windows(own, other, near, far, weight, sums, cells)
    hidden = forward[...]
    weights = (w_high[...], w_low[...])
    image = (x_high[...], x_low[...])
    at = lax.broadcasted_iota(jnp.int32, (64, FLAT), 1)
    block = lax.axis_index("rows") // 2
    across = at % STEP < BLOCK
    inside = across & (at >= STEP) & (at < (ROWS + 1) * STEP)
    top = jnp.where(block == 0, STEP, 0)
    bottom = jnp.where(block == 3, (ROWS + 1) * STEP, (ROWS + 2) * STEP)
    around = across & (at >= top) & (at < bottom)
    sigma = 1.0 / (1.0 + jnp.exp(-hidden))
    active = jnp.where(inside, hidden * sigma, 0.0)
    slope = sigma * (1.0 + hidden * (1.0 - sigma))
    gradient = grad * slope

    def stack(values, offset):
        for t in range(9):
            shift = ((t // 3) * STEP + t % 3 + offset) % FLAT
            high, low = halves(pltpu.roll(values, shift, 1) if shift else values)
            g_high[t * 64 : t * 64 + 64, :] = high
            g_low[t * 64 : t * 64 + 64, :] = low
        return g_high[...], g_low[...]

    moved = stack(jnp.where(inside, gradient, 0.0), 0)
    into = product(moved, image, NT)
    for t in range(9):
        for h in range(2):
            for j in range(2):
                out[pl.ds((t * 2 + h) * 2 + j, 32, stride=BACK), :] = into[
                    t * 64 + j * 32 : t * 64 + j * 32 + 32, h * 128 : h * 128 + 128
                ]
    shifts = [0, 1, STEP, STEP + 1]
    spread = jnp.concatenate([pltpu.roll(active, s, 1) if s else active for s in shifts], axis=0)
    onto = product(halves(spread), parts, NN)
    for t in range(9):
        at, kind = shifts.index(shift_of(t)) * 64, kind_of(t)
        for j in range(2):
            out[pl.ds(36 + t * 2 + j, 32, stride=BACK), :] = onto[
                at + j * 32 : at + j * 32 + 32, kind * 128 : kind * 128 + 128
            ]
    back = product(weights, stack(jnp.where(around, gradient, 0.0), -2 * STEP), TN)
    half = ROWS // 2 * STEP
    first = lax.axis_index("rows") % 2 == 0
    upper, lower = back[:, 0:256], pltpu.roll(back, FLAT - half, 1)[:, 0:256]
    for dst, part in (
        (mine, jnp.where(first, upper, lower)),
        (theirs, jnp.where(first, lower, upper)),
    ):
        for d in range(32):
            for q in range(2):
                dst[pl.ds(d * 16 + q * 8, 8), :] = part[d * 8 : d * 8 + 8, q * 128 : q * 128 + 128]
    blank = jnp.zeros((2, 128), F32)
    for d in range(32):
        out[pl.ds(d * BACK + 54, 2), :] = blank


def weights_kernel(scale, recv, mixed, total):
    mixed[...] = jnp.zeros_like(mixed)
    for core in range(2):
        each = recv[core]
        for block in range(1, 16):
            each = each + recv[2 * block + core]
        total[...] = each * scale
        for j in range(2):
            mixed[pl.ds(2 * core + j, 27, stride=4), :] = total[pl.ds(j, 27, stride=2), :]


def add_kernel(own, other, total):
    total[...] = own[...] + other[...]


def final_kernel(own, other, into, onto):
    first = lax.axis_index("rows") % 2 == 0
    sums = (
        jnp.where(first, own[...], other[...]),
        jnp.where(first, other[...], own[...]),
    )
    for k in range(27):
        tile = jnp.concatenate([x[4 * k : 4 * k + 4] for x in sums], axis=0)
        if k < 18:
            into[k // 2, :, (k % 2) * 128 : (k % 2) * 128 + 128] = tile
        else:
            onto[k - 18] = tile


def image_kernel(recv, out, image, line):
    image[...] = jnp.zeros_like(image)
    for block in range(16):
        start = 127 + BLOCK * block
        for q in range(2):
            at = slice(q * 8, q * 8 + 8)
            line[:, q * 128 : q * 128 + 128] = recv[2 * block, at, :] + recv[2 * block + 1, at, :]
        for r in range(ROWS // 2):
            image[r, :, start : start + STEP] += line[:, r * STEP : (r + 1) * STEP]
    for r in range(ROWS // 2):
        out[r] = image[r, :, 128:384]


def shape(*dims, dtype=F32):
    return jax.ShapeDtypeStruct(dims, dtype)


def call(kernel, outs, args, scratch=(), flops=10**6, moved=10**6, specs=None, grant=GRANT):
    return pl.pallas_call(
        kernel,
        out_shape=outs,
        in_specs=specs or [FULL] * args,
        out_specs=jax.tree.map(lambda _: FULL, outs),
        scratch_shapes=list(scratch),
        compiler_params=pltpu.CompilerParams(vmem_limit_bytes=grant),
        cost_estimate=pl.CostEstimate(flops=flops, bytes_accessed=moved, transcendentals=0),
    )


def partner(n, by=1):
    return [(i, i ^ by) for i in range(n)]


def beside(n):
    return [(i, i + 1) for i in range(1, n - 1, 2)] + [(i, i - 1) for i in range(2, n, 2)]


def inward(n):
    return [(i, i + 2) for i in range(1, n - 2, 2)] + [(i, i - 2) for i in range(2, n, 2)]


def mirrored(n):
    return [(i, (n - 2 - i + 2 * (i % 2)) % n) for i in range(n)]


def local(features, weight_in, weight_out, cotangent):
    scale = (4.0 * features.shape[1] * lax.axis_size("rows") * features.shape[2]) ** (-0.5)
    flat = pltpu.VMEM((8, FLAT), F32)

    lines = jnp.transpose(features, (1, 0, 2))
    taps = jnp.transpose(weight_in, (1, 2, 0, 3)).reshape(9, 8, 256)
    edge, packed = call(
        prepare_kernel, (shape(80, 128), shape(32, PACK, 128)), 3,
        [
            pltpu.VMEM((2, 8, 256), F32), pltpu.VMEM((3, 16, 128), F32),
            pltpu.VMEM((9, 8, 256), F32), pltpu.VMEM((2, PACK, 128), F32),
            pltpu.SemaphoreType.DMA((3,)),
        ],
        specs=[pl.BlockSpec(memory_space=pltpu.HBM)] * 3, grant=MOST,
    )(lines, cotangent, taps)
    near = lax.ppermute(edge, "rows", beside(8))
    far = lax.ppermute(edge, "rows", inward(8))
    other = lax.ppermute(lines, "rows", partner(8))
    other_c = lax.ppermute(cotangent, "rows", partner(8))
    kernels = lax.all_to_all(packed, "chan", 0, 0, tiled=True)
    near, far, other, other_c, kernels = lax.optimization_barrier((near, far, other, other_c, kernels))
    packed = call(pack_kernel, shape(32, 32, 128), 4, [pltpu.VMEM((ROWS + 4, 8, 512), F32), flat])(
        lines, other, near, far
    )
    recv = lax.all_to_all(packed, "chan", 0, 0, tiled=True)

    tall, side = call(column_kernel, (shape(FINE, 16, 128), shape(FINE + 2, 128)), 4)(
        cotangent, other_c, near, far
    )
    near_side = lax.ppermute(side, "chan", beside(32))
    other_tall = lax.ppermute(tall, "chan", partner(32))
    far_side = lax.ppermute(near_side, "chan", partner(32))
    forward = call(
        hidden_kernel,
        (
            shape(64, FLAT), shape(256, FLAT, dtype=BF16), shape(256, FLAT, dtype=BF16),
            shape(576, 256, dtype=BF16), shape(576, 256, dtype=BF16),
        ),
        2, (), 5 * 10**9, 5 * 10**6,
    )(recv.reshape(1024, 128), kernels.reshape(32 * PACK, 128))
    sent, own, given = call(
        main_kernel, (shape(32 * BACK, 128), shape(512, 128), shape(512, 128)), 10,
        [
            pltpu.VMEM((FINE, 48, 128), F32), pltpu.VMEM((FLAT, 512), F32),
            pltpu.VMEM((576, FLAT), BF16), pltpu.VMEM((576, FLAT), BF16),
        ],
        10**9, 5 * 10**6,
    )(
        *forward, tall, other_tall, near_side, far_side,
        jnp.transpose(weight_out, (1, 2, 0, 3)).reshape(2304, 128),
    )
    given = lax.ppermute(given, "rows", partner(8))
    back = lax.all_to_all(sent.reshape(32, BACK, 128), "chan", 0, 0, tiled=True)
    moved, back = lax.optimization_barrier((own + given, back))
    mixed = call(lambda *refs: weights_kernel(scale, *refs), shape(112, 128), 1, [pltpu.VMEM((56, 128), F32)])(
        back
    )
    moved, mixed = lax.optimization_barrier((moved, mixed))
    image = lax.all_to_all(moved.reshape(32, 16, 128), "chan", 0, 0, tiled=True)
    opposite = lax.ppermute(mixed, "rows", partner(8, 2))
    mixed = call(add_kernel, shape(112, 128), 2, (), 10**10, 10**7)(mixed, opposite)
    opposite = lax.ppermute(mixed, "rows", mirrored(8))
    mixed = mixed + opposite
    counter = lax.ppermute(mixed, "rows", partner(8))
    rows = call(
        image_kernel, shape(12, 8, 256), 1,
        [pltpu.VMEM((12, 8, 512), F32), pltpu.VMEM((8, 256), F32)],
    )(image)
    rows, counter = lax.optimization_barrier((rows, counter))
    into, onto = call(final_kernel, (shape(9, 8, 256), shape(9, 8, 128)), 2)(mixed, counter)
    grad_image = jnp.transpose(rows, (1, 0, 2))
    grad_in = jnp.transpose(into.reshape(3, 3, 8, 256), (2, 0, 1, 3))
    grad_out = jnp.transpose(onto.reshape(3, 3, 8, 128), (2, 0, 1, 3))
    return (grad_image, grad_in, grad_out)


def solution(mesh):
    return jax.shard_map(
        local,
        mesh=mesh,
        in_specs=(
            P("chan", "rows", None),
            P("chan", None, None, None),
            P(),
            P("rows", "chan", None),
        ),
        out_specs=(
            P("chan", "rows", None),
            P("chan", None, None, None),
            P("chan", None, None, None),
        ),
        check_vma=False,
    )
```

```python
import jax
import jax.numpy as jnp
from jax import lax
from jax.experimental import pallas as pl
from jax.experimental.pallas import tpu as pltpu
from jax.sharding import PartitionSpec as P

BLOCK = 16
STEP = BLOCK + 2
ROWS = 24
FINE = 2 * ROWS + 6
FLAT = 512
PACK = 40
BACK = 56
F32, BF16 = jnp.float32, jnp.bfloat16
GRANT, MOST = 20 * 1024 * 1024, 60 * 1024 * 1024
FULL = pl.BlockSpec(memory_space=pltpu.VMEM)


def halves(x):
    high = x.astype(BF16)
    return high, (x - high.astype(F32)).astype(BF16)


def product(a, b, dims):
    def one(x, y):
        return lax.dot_general(x, y, (dims, ((), ())), preferred_element_type=F32)

    return one(a[0], b[0]) + (one(a[0], b[1]) + one(a[1], b[0]))


NN, NT, TN = ((1,), (0,)), ((1,), (1,)), ((0,), (0,))


def prepare_kernel(features, cotangent, weight, edge, packed, lines, cells, taps, part, sems):
    parity = lax.axis_index("rows") % 2
    half = ROWS // 2
    copies = [
        pltpu.make_async_copy(weight, taps, sems.at[0]),
        pltpu.make_async_copy(features.at[pl.ds((half - 2) * parity, 2)], lines, sems.at[1]),
        pltpu.make_async_copy(cotangent.at[pl.ds((ROWS - 3) * parity, 3)], cells, sems.at[2]),
    ]
    for copy in copies:
        copy.start()
    part[...] = jnp.zeros_like(part)
    for copy in copies:
        copy.wait()
    for k in range(2):
        for h in range(2):
            at = (2 * k + h) * 8
            edge[at : at + 8, :] = lines[k, :, h * 128 : h * 128 + 128]
    for k in range(3):
        edge[32 + k * 16 : 48 + k * 16, :] = cells[k]
    for t in range(9):
        rows = jnp.where(parity == 0, taps[t, 0:4, :], taps[t, 4:8, :])
        for core in range(2):
            for h in range(2):
                at = (t * 2 + h) * 2
                part[core, at : at + 2, :] = rows[
                    2 * core : 2 * core + 2, h * 128 : h * 128 + 128
                ]
    for core in range(2):
        tile = part[core]
        for block in range(16):
            packed[2 * block + core] = tile


def pack_kernel(own, other, near, far, out, image, line):
    parity = lax.axis_index("rows") % 2
    image[...] = jnp.zeros_like(image)
    line[...] = jnp.zeros_like(line)
    inner = slice(128, 384)
    half = ROWS // 2
    for i in range(half):
        image[2 + half * parity + i, :, inner] = own[i]
        image[2 + half * (1 - parity) + i, :, inner] = other[i]
    for edge, at in ((near, parity), (far, 1 - parity)):
        for k in range(2):
            for h in range(2):
                rows = (2 * k + h) * 8
                image[(ROWS + 2) * at + k, :, 128 + h * 128 : 256 + h * 128] = edge[rows : rows + 8]
    for block in range(16):
        start = 127 + BLOCK * block
        for r in range(ROWS + 4):
            line[:, r * STEP : (r + 1) * STEP] = image[r, :, start : start + STEP]
        for q in range(4):
            tile = line[:, q * 128 : (q + 1) * 128]
            out[2 * block, q * 8 : q * 8 + 8, :] = tile
            out[2 * block + 1, q * 8 : q * 8 + 8, :] = tile


def column_kernel(own, other, near, far, tall, side):
    parity = lax.axis_index("rows") % 2
    core = lax.axis_index("chan") % 2
    tall[pl.ds(3 + ROWS * parity, ROWS)] = own[...]
    tall[pl.ds(3 + ROWS * (1 - parity), ROWS)] = other[...]
    for edge, at in ((near, parity), (far, 1 - parity)):
        for k in range(3):
            tall[(2 * ROWS + 3) * at + k] = edge[32 + 16 * k : 48 + 16 * k]
    for r in range(FINE):
        line = tall[r]
        side[r : r + 1, :] = jnp.where(core == 0, line[0:1], line[15:16])
    side[FINE : FINE + 2, :] = jnp.zeros((2, 128), F32)


def windows(own, other, near, far, weight, sums, image):
    core = lax.axis_index("chan") % 2
    group = 2 * (lax.axis_index("rows") % 2) + core
    image[:, pl.ds(pl.multiple_of(8 + 16 * core, 8), 16), :] = own[...]
    image[:, pl.ds(pl.multiple_of(24 - 16 * core, 8), 16), :] = other[...]
    left = jnp.where(core == 0, near[...], far[...])
    right = jnp.where(core == 0, far[...], near[...])
    for r in range(FINE):
        image[r, 7:8, :] = left[r : r + 1]
        image[r, 40:41, :] = right[r : r + 1]
    sums[...] = jnp.zeros_like(sums)

    def cells(r, start, count):
        return image[r, pl.ds(start, count, stride=2), :]

    def pairs(r, start, count):
        return cells(r, start, count) + cells(r, start + 1, count)

    even = [pairs(r, 7, 17) for r in range(FINE)]
    odd = [pairs(r, 8, 16) for r in range(FINE)]
    for r in range(ROWS + 3):
        at = r * STEP
        sums[at : at + 17, 0:128] = even[2 * r] + even[2 * r + 1]
        sums[at : at + 16, 128:256] = odd[2 * r] + odd[2 * r + 1]
        if r < ROWS + 2:
            sums[at : at + 17, 256:384] = even[2 * r + 1] + even[2 * r + 2]
            sums[at : at + 16, 384:512] = odd[2 * r + 1] + odd[2 * r + 2]
    high, low = halves(sums[...])
    total = None
    for kind in range(4):
        lanes = slice(kind * 128, (kind + 1) * 128)
        taps = [t for t in range(9) if kind_of(t) == kind]
        left_side = jnp.concatenate(
            [
                weight[pl.ds(t * 256 + 2 * group + j, 32, stride=8), :]
                for t in taps
                for j in range(2)
            ],
            axis=0,
        )
        each = product(halves(left_side), (high[:, lanes], low[:, lanes]), NT)
        for i, t in enumerate(taps):
            term = each[i * 64 : (i + 1) * 64]
            if shift_of(t):
                term = pltpu.roll(term, FLAT - shift_of(t), 1)
            total = term if total is None else total + term
    return (high, low), total


def kind_of(t):
    return 2 * (t // 3 == 1) + (t % 3 == 1)


def shift_of(t):
    return STEP * (t // 3 == 0) + (t % 3 == 0)


def hidden_kernel(recv, kernels, result, x_high, x_low, w_high, w_low):
    for pair in range(16):
        for q in range(4):
            tile = jnp.concatenate(
                [recv[pl.ds((2 * pair + i) * 32 + q * 8, 8), :] for i in range(2)], axis=0
            )
            high, low = halves(tile)
            x_high[pair * 16 : pair * 16 + 16, q * 128 : q * 128 + 128] = high
            x_low[pair * 16 : pair * 16 + 16, q * 128 : q * 128 + 128] = low
    for t in range(9):
        for h in range(2):
            tile = jnp.concatenate(
                [kernels[pl.ds((t * 2 + h) * 2 + j, 32, stride=PACK), :] for j in range(2)], axis=0
            )
            high, low = halves(tile)
            w_high[t * 64 : t * 64 + 64, h * 128 : h * 128 + 128] = high
            w_low[t * 64 : t * 64 + 64, h * 128 : h * 128 + 128] = low
    weights = (w_high[...], w_low[...])
    image = (x_high[...], x_low[...])
    each = product(weights, image, NN)
    hidden = each[0:64]
    for t in range(1, 9):
        hidden = hidden + pltpu.roll(each[t * 64 : t * 64 + 64], FLAT - ((t // 3) * STEP + t % 3), 1)
    result[...] = hidden


def stack(values, offset, g_high, g_low):
    for t in range(9):
        shift = ((t // 3) * STEP + t % 3 + offset) % FLAT
        high, low = halves(pltpu.roll(values, shift, 1) if shift else values)
        g_high[t * 64 : t * 64 + 64, :] = high
        g_low[t * 64 : t * 64 + 64, :] = low
    return g_high[...], g_low[...]


def main_kernel(
    forward, x_high, x_low, own, other, near, far, weight, out, gradient_out,
    cells, sums, g_high, g_low,
):
    parts, grad = windows(own, other, near, far, weight, sums, cells)
    hidden = forward[...]
    image = (x_high[...], x_low[...])
    at = lax.broadcasted_iota(jnp.int32, (64, FLAT), 1)
    block = lax.axis_index("rows") // 2
    across = at % STEP < BLOCK
    inside = across & (at >= STEP) & (at < (ROWS + 1) * STEP)
    top = jnp.where(block == 0, STEP, 0)
    bottom = jnp.where(block == 3, (ROWS + 1) * STEP, (ROWS + 2) * STEP)
    around = across & (at >= top) & (at < bottom)
    sigma = 1.0 / (1.0 + jnp.exp(-hidden))
    active = jnp.where(inside, hidden * sigma, 0.0)
    slope = sigma * (1.0 + hidden * (1.0 - sigma))
    gradient = grad * slope

    moved = stack(jnp.where(inside, gradient, 0.0), 0, g_high, g_low)
    into = product(moved, image, NT)
    for t in range(9):
        for h in range(2):
            for j in range(2):
                out[pl.ds((t * 2 + h) * 2 + j, 32, stride=BACK), :] = into[
                    t * 64 + j * 32 : t * 64 + j * 32 + 32, h * 128 : h * 128 + 128
                ]
    shifts = [0, 1, STEP, STEP + 1]
    spread = jnp.concatenate([pltpu.roll(active, s, 1) if s else active for s in shifts], axis=0)
    onto = product(halves(spread), parts, NN)
    for t in range(9):
        at, kind = shifts.index(shift_of(t)) * 64, kind_of(t)
        for j in range(2):
            out[pl.ds(36 + t * 2 + j, 32, stride=BACK), :] = onto[
                at + j * 32 : at + j * 32 + 32, kind * 128 : kind * 128 + 128
            ]
    gradient_out[...] = jnp.where(around, gradient, 0.0)
    blank = jnp.zeros((2, 128), F32)
    for d in range(32):
        out[pl.ds(d * BACK + 54, 2), :] = blank


def back_kernel(gradient, w_high, w_low, mine, theirs, g_high, g_low):
    weights = (w_high[...], w_low[...])
    back = product(weights, stack(gradient[...], -2 * STEP, g_high, g_low), TN)
    half = ROWS // 2 * STEP
    first = lax.axis_index("rows") % 2 == 0
    upper, lower = back[:, 0:256], pltpu.roll(back, FLAT - half, 1)[:, 0:256]
    for dst, part in (
        (mine, jnp.where(first, upper, lower)),
        (theirs, jnp.where(first, lower, upper)),
    ):
        for d in range(32):
            for q in range(2):
                dst[pl.ds(d * 16 + q * 8, 8), :] = part[d * 8 : d * 8 + 8, q * 128 : q * 128 + 128]


def weights_kernel(scale, recv, mixed, total):
    mixed[...] = jnp.zeros_like(mixed)
    for core in range(2):
        each = recv[core]
        for block in range(1, 16):
            each = each + recv[2 * block + core]
        total[...] = each * scale
        for j in range(2):
            mixed[pl.ds(2 * core + j, 27, stride=4), :] = total[pl.ds(j, 27, stride=2), :]


def add_kernel(own, other, total):
    total[...] = own[...] + other[...]


def final_kernel(own, other, into, onto):
    first = lax.axis_index("rows") % 2 == 0
    sums = (
        jnp.where(first, own[...], other[...]),
        jnp.where(first, other[...], own[...]),
    )
    for k in range(27):
        tile = jnp.concatenate([x[4 * k : 4 * k + 4] for x in sums], axis=0)
        if k < 18:
            into[k // 2, :, (k % 2) * 128 : (k % 2) * 128 + 128] = tile
        else:
            onto[k - 18] = tile


def image_kernel(recv, out, image, line):
    image[...] = jnp.zeros_like(image)
    for block in range(16):
        start = 127 + BLOCK * block
        for q in range(2):
            at = slice(q * 8, q * 8 + 8)
            line[:, q * 128 : q * 128 + 128] = recv[2 * block, at, :] + recv[2 * block + 1, at, :]
        for r in range(ROWS // 2):
            image[r, :, start : start + STEP] += line[:, r * STEP : (r + 1) * STEP]
    for r in range(ROWS // 2):
        out[r] = image[r, :, 128:384]


def shape(*dims, dtype=F32):
    return jax.ShapeDtypeStruct(dims, dtype)


def call(kernel, outs, args, scratch=(), flops=10**6, moved=10**6, specs=None, grant=GRANT):
    return pl.pallas_call(
        kernel,
        out_shape=outs,
        in_specs=specs or [FULL] * args,
        out_specs=jax.tree.map(lambda _: FULL, outs),
        scratch_shapes=list(scratch),
        compiler_params=pltpu.CompilerParams(vmem_limit_bytes=grant),
        cost_estimate=pl.CostEstimate(flops=flops, bytes_accessed=moved, transcendentals=0),
    )


def partner(n, by=1):
    return [(i, i ^ by) for i in range(n)]


def beside(n):
    return [(i, i + 1) for i in range(1, n - 1, 2)] + [(i, i - 1) for i in range(2, n, 2)]


def inward(n):
    return [(i, i + 2) for i in range(1, n - 2, 2)] + [(i, i - 2) for i in range(2, n, 2)]


def mirrored(n):
    return [(i, (n - 2 - i + 2 * (i % 2)) % n) for i in range(n)]


def local(features, weight_in, weight_out, cotangent):
    scale = (4.0 * features.shape[1] * lax.axis_size("rows") * features.shape[2]) ** (-0.5)
    flat = pltpu.VMEM((8, FLAT), F32)

    lines = jnp.transpose(features, (1, 0, 2))
    taps = jnp.transpose(weight_in, (1, 2, 0, 3)).reshape(9, 8, 256)
    edge, packed = call(
        prepare_kernel, (shape(80, 128), shape(32, PACK, 128)), 3,
        [
            pltpu.VMEM((2, 8, 256), F32), pltpu.VMEM((3, 16, 128), F32),
            pltpu.VMEM((9, 8, 256), F32), pltpu.VMEM((2, PACK, 128), F32),
            pltpu.SemaphoreType.DMA((3,)),
        ],
        specs=[pl.BlockSpec(memory_space=pltpu.HBM)] * 3, grant=MOST,
    )(lines, cotangent, taps)
    near = lax.ppermute(edge, "rows", beside(8))
    far = lax.ppermute(edge, "rows", inward(8))
    other = lax.ppermute(lines, "rows", partner(8))
    other_c = lax.ppermute(cotangent, "rows", partner(8))
    kernels = lax.all_to_all(packed, "chan", 0, 0, tiled=True)
    near, far, other, other_c, kernels = lax.optimization_barrier((near, far, other, other_c, kernels))
    packed = call(pack_kernel, shape(32, 32, 128), 4, [pltpu.VMEM((ROWS + 4, 8, 512), F32), flat])(
        lines, other, near, far
    )
    recv = lax.all_to_all(packed, "chan", 0, 0, tiled=True)

    tall, side = call(column_kernel, (shape(FINE, 16, 128), shape(FINE + 2, 128)), 4)(
        cotangent, other_c, near, far
    )
    near_side = lax.ppermute(side, "chan", beside(32))
    other_tall = lax.ppermute(tall, "chan", partner(32))
    far_side = lax.ppermute(near_side, "chan", partner(32))
    forward = call(
        hidden_kernel,
        (
            shape(64, FLAT), shape(256, FLAT, dtype=BF16), shape(256, FLAT, dtype=BF16),
            shape(576, 256, dtype=BF16), shape(576, 256, dtype=BF16),
        ),
        2, (), 5 * 10**9, 5 * 10**6,
    )(recv.reshape(1024, 128), kernels.reshape(32 * PACK, 128))
    hidden, x_high, x_low, w_high, w_low = forward
    stacks = [pltpu.VMEM((576, FLAT), BF16), pltpu.VMEM((576, FLAT), BF16)]
    sent, gradient = call(
        main_kernel, (shape(32 * BACK, 128), shape(64, FLAT)), 8,
        [pltpu.VMEM((FINE, 48, 128), F32), pltpu.VMEM((FLAT, 512), F32)] + stacks, 10**9, 5 * 10**6,
    )(
        hidden, x_high, x_low, tall, other_tall, near_side, far_side,
        jnp.transpose(weight_out, (1, 2, 0, 3)).reshape(2304, 128),
    )
    own, given = call(back_kernel, (shape(512, 128), shape(512, 128)), 3, stacks, 5 * 10**9, 3 * 10**6)(
        gradient, w_high, w_low
    )
    given = lax.ppermute(given, "rows", partner(8))
    back = lax.all_to_all(sent.reshape(32, BACK, 128), "chan", 0, 0, tiled=True)
    moved, back = lax.optimization_barrier((own + given, back))
    mixed = call(lambda *refs: weights_kernel(scale, *refs), shape(112, 128), 1, [pltpu.VMEM((56, 128), F32)])(
        back
    )
    moved, mixed = lax.optimization_barrier((moved, mixed))
    image = lax.all_to_all(moved.reshape(32, 16, 128), "chan", 0, 0, tiled=True)
    opposite = lax.ppermute(mixed, "rows", partner(8, 2))
    mixed = call(add_kernel, shape(112, 128), 2, (), 10**10, 10**7)(mixed, opposite)
    opposite = lax.ppermute(mixed, "rows", mirrored(8))
    mixed = mixed + opposite
    counter = lax.ppermute(mixed, "rows", partner(8))
    rows = call(
        image_kernel, shape(12, 8, 256), 1,
        [pltpu.VMEM((12, 8, 512), F32), pltpu.VMEM((8, 256), F32)],
    )(image)
    rows, counter = lax.optimization_barrier((rows, counter))
    into, onto = call(final_kernel, (shape(9, 8, 256), shape(9, 8, 128)), 2)(mixed, counter)
    grad_image = jnp.transpose(rows, (1, 0, 2))
    grad_in = jnp.transpose(into.reshape(3, 3, 8, 256), (2, 0, 1, 3))
    grad_out = jnp.transpose(onto.reshape(3, 3, 8, 128), (2, 0, 1, 3))
    return (grad_image, grad_in, grad_out)


def solution(mesh):
    return jax.shard_map(
        local,
        mesh=mesh,
        in_specs=(
            P("chan", "rows", None),
            P("chan", None, None, None),
            P(),
            P("rows", "chan", None),
        ),
        out_specs=(
            P("chan", "rows", None),
            P("chan", None, None, None),
            P("chan", None, None, None),
        ),
        check_vma=False,
    )
```
